128 devices in a mesh: dp: 32 (over y, z, core), tp: 4 (over x).
Axes of the slice: x: 4, y: 4, z: 4, core: 2. Of those that a mesh axis runs over, the one named last changes fastest.
Arguments:
- latent_cache: bfloat16 [256, 448, 576], P('dp'), may hold values from -5 to 5
- lengths: int32 [256], replicated, may hold values from 1 to 446, as said below
- slot_moves: int32 [2, 32, 2], replicated, may hold values from 0 to 7, as said below
- hidden_in: bfloat16 [2, 256, 7168], P(None, 'dp', 'tp'), may hold values from -7.2 to 7.2
- queries: bfloat16 [2, 256, 128, 576], P(None, 'dp', 'tp'), may hold values from -6 to 6
- latent_weight: bfloat16 [7168, 576], P('tp'), may hold values from -0.0625 to 0.0625
- value_up_projection: bfloat16 [128, 512, 128], P('tp'), may hold values from -0.25 to 0.25
- out_weight: bfloat16 [16384, 7168], P('dp', 'tp'), may hold values from -0.046875 to 0.046875
- post_gain: float32 [7168], P('tp'), may hold values from 0.1 to 1.9
- gate_projection_matrix: bfloat16 [7168, 18432], P('tp', 'dp'), may hold values from -0.0625 to 0.0625
- up_weight: bfloat16 [7168, 18432], P('tp', 'dp'), may hold values from -0.0625 to 0.0625
- down_weight: bfloat16 [18432, 7168], P('dp', 'tp'), may hold values from -0.046875 to 0.046875
Outputs:
- layer_out: bfloat16 [2, 256, 7168], P(None, 'dp', 'tp')
- final_cache: bfloat16 [256, 448, 576], P('dp')
- final_lengths: int32 [256], replicated
The draws below stay inside these ranges and needn't reach their ends.
Inputs may be any that keep to these rules, and one draw needn't show every extreme that they name: `lengths`: the largest length is 446 in every draw. `slot_moves`: for each step and group the two local slots differ.
All inputs are finite; a program needn't handle non-finite values.
Results may differ from the reference program's by a relative error of at most 0.015.
Values may be sent and summed in bfloat16 or wider, within the bound.
A program may use at most 128 MiB of HBM per device.

```python
import jax
import jax.numpy as jnp
from jax import lax

D = 7168
H = 128
KVR = 512
ROPE = 64
HD = 128
FF = 18432
LAT = 576
ROWS_DEV = 8
CAP = 448
STEPS = 2
ROWS = 256
N_DP = 32


def draw_latent_cache(key, part):
    key = jax.random.fold_in(key, 12)
    shape = (ROWS, CAP, LAT)
    values = jax.random.truncated_normal(key, -5.0, 5.0, shape, jnp.float32)
    return values.astype(jnp.bfloat16)


def draw_queries(key, part):
    key = jax.random.fold_in(key, 13)
    first_key = jax.random.fold_in(key, 0)
    shape = (STEPS, ROWS, H, LAT)
    values = jax.random.truncated_normal(first_key, -6.0, 6.0, shape, jnp.float32)
    return values.astype(jnp.bfloat16)


def draw_hidden_in(key, part):
    key = jax.random.fold_in(key, 11)
    first_key = jax.random.fold_in(key, 0)
    shape = (STEPS, ROWS, D)
    column_ramp = 0.6 * 3.0 ** (jnp.arange(D, dtype=jnp.float32) / D)
    values = jax.random.truncated_normal(first_key, -4.0, 4.0, shape, jnp.float32) * column_ramp
    return values.astype(jnp.bfloat16)


def draw_lengths(key, part):
    key = jax.random.fold_in(key, 14)
    first_key, second_key, third_key = jax.random.split(key, 3)
    spread = jax.random.randint(first_key, (ROWS,), 0, CAP - 2)
    divider = jax.random.randint(second_key, (ROWS,), 1, 9)
    values = 1 + spread // divider
    longest = jax.random.randint(third_key, (), 0, ROWS)
    return jnp.where(jnp.arange(ROWS) == longest, CAP - 2, values).astype(jnp.int32)


def draw_slot_moves(key, part):
    key = jax.random.fold_in(key, 15)
    first_key, second_key = jax.random.split(key)
    first_slot = jax.random.randint(first_key, (STEPS, N_DP), 0, ROWS_DEV)
    offset = jax.random.randint(second_key, (STEPS, N_DP), 1, ROWS_DEV)
    second_slot = (first_slot + offset) % ROWS_DEV
    return jnp.stack([first_slot, second_slot], axis=-1).astype(jnp.int32)


def steps_of(key, dims, cuts, low, top_value):
    loudness = 1.0
    for dim, blocks in cuts:
        steps = jax.random.uniform(jax.random.fold_in(jax.random.fold_in(key, 6), dim), (blocks,), jnp.float32, low / len(cuts), top_value / len(cuts))
        loudness = loudness * jnp.repeat(jnp.exp(steps), dims[dim] // blocks).reshape((-1,) + (1,) * (len(dims) - 1 - dim))
    return loudness


def scatter_about(key, dims, scale, bound, shards=(), held_as=jnp.bfloat16):
    result = scale * jax.random.normal(key, dims, jnp.float32)
    if shards:
        result = result * steps_of(key, dims, shards, -0.22, 0.18)
    return jnp.clip(result, -bound, bound).astype(held_as)


def setup_inputs(seed: int = 0) -> dict:
    seeds = jax.random.split(jax.random.key(seed), 13)
    latent_cache = draw_latent_cache(jax.random.fold_in(seeds[12], 71), 0)
    lengths = draw_lengths(jax.random.fold_in(seeds[12], 71), 0)
    slot_moves = draw_slot_moves(jax.random.fold_in(seeds[12], 71), 0)
    hidden_in = draw_hidden_in(jax.random.fold_in(seeds[12], 71), 0)
    queries = draw_queries(jax.random.fold_in(seeds[12], 71), 0)
    latent_weight = scatter_about(seeds[5], (D, LAT), D ** -0.5, 0.0625, ((0, 4),))
    value_up_projection = scatter_about(seeds[6], (H, KVR, HD), KVR ** -0.5, 0.25, ((0, 4),))
    out_weight = scatter_about(seeds[7], (H * HD, D), (H * HD) ** -0.5, 0.046875, ((0, 32), (1, 4)))
    post_gain = jnp.clip(1.0 + 0.18 * jax.random.normal(seeds[8], (D,), jnp.float32), 0.1, 1.9)
    gate_projection_matrix = scatter_about(seeds[9], (D, FF), D ** -0.5, 0.0625, ((0, 4), (1, 32)))
    up_weight = scatter_about(seeds[10], (D, FF), D ** -0.5, 0.0625, ((0, 4), (1, 32)))
    down_weight = scatter_about(seeds[11], (FF, D), FF ** -0.5, 0.046875, ((0, 32), (1, 4)))
    return dict(latent_cache=latent_cache, lengths=lengths, slot_moves=slot_moves, hidden_in=hidden_in, queries=queries, latent_weight=latent_weight, value_up_projection=value_up_projection, out_weight=out_weight, post_gain=post_gain, gate_projection_matrix=gate_projection_matrix, up_weight=up_weight, down_weight=down_weight)


epsilon = 1e-06

def source_slots(moves_step, groups, per_group):
    group_base = jnp.arange(groups, dtype=jnp.int32) * per_group
    right_slot = group_base + moves_step[:, 0].astype(jnp.int32)
    left_slot = group_base + moves_step[:, 1].astype(jnp.int32)
    source = jnp.arange(groups * per_group, dtype=jnp.int32)
    source = source.at[right_slot].set(jnp.roll(left_slot, -1))
    source = source.at[left_slot].set(jnp.roll(right_slot, 1))
    return source

def rotate_pairs(rotary, positions):
    half_width = rotary.shape[-1] // 2
    frequencies = 10000.0 ** (-2.0 * jnp.arange(half_width, dtype=jnp.float32) / rotary.shape[-1])
    angles = positions.astype(jnp.float32)[:, None] * frequencies[None, :]
    cosine = jnp.cos(angles)
    sine_part = jnp.sin(angles)
    front_half = rotary[:, :half_width]
    back_half = rotary[:, half_width:]
    return jnp.concatenate([front_half * cosine - back_half * sine_part, back_half * cosine + front_half * sine_part], axis=1)

def finish_key(latent, positions):
    content = latent[:, :KVR]
    content = content * lax.rsqrt(lax.optimization_barrier(jnp.mean(content * content, axis=1, keepdims=True)) + epsilon)
    return jnp.concatenate([content, rotate_pairs(latent[:, KVR:], positions)], axis=1).astype(jnp.bfloat16)

def attend_slot(operands):
    query_row_block, key_rows, live_count = operands
    query_wide = query_row_block.astype(jnp.float32)
    key_wide = key_rows.astype(jnp.float32)
    scores = jnp.einsum('hl,tl->ht', query_wide, key_wide) * (HD + ROPE) ** (-0.5)
    visible = jnp.arange(CAP, dtype=jnp.int32) < live_count
    scores = jnp.where(visible[None, :], scores, -1e+30)
    peak_score = lax.optimization_barrier(jnp.max(scores, axis=1, keepdims=True))
    powers = jnp.exp(scores - peak_score)
    weights = (powers / lax.optimization_barrier(jnp.sum(powers, axis=1, keepdims=True))).astype(jnp.bfloat16)
    return jnp.einsum('ht,tk->hk', weights.astype(jnp.float32), key_wide[:, :KVR]).astype(jnp.bfloat16)

def reference(latent_cache, lengths, slot_moves, hidden_in, queries, latent_weight, value_up_projection, out_weight, post_gain, gate_projection_matrix, up_weight, down_weight):
    outputs = []
    for step_index in range(STEPS):
        source = source_slots(slot_moves[step_index], N_DP, ROWS_DEV)
        latent_cache = latent_cache[source]
        held_lengths = lengths[source]
        tokens = hidden_in[step_index]
        tokens_wide = tokens.astype(jnp.float32)
        latent = jnp.dot(tokens, latent_weight, preferred_element_type=jnp.float32)
        latent = latent * lax.rsqrt(lax.optimization_barrier(jnp.mean(tokens_wide * tokens_wide, axis=1)) + epsilon)[:, None]
        fresh_key = finish_key(latent, held_lengths)
        latent_cache = latent_cache.at[jnp.arange(ROWS, dtype=jnp.int32), held_lengths].set(fresh_key)
        lengths = held_lengths + 1
        per_head_latent_vector = lax.map(attend_slot, (queries[step_index], latent_cache, lengths))
        head_output_rows = jnp.einsum('gfe,feu->gfu', per_head_latent_vector.astype(jnp.float32), value_up_projection.astype(jnp.float32))
        head_output_rows = head_output_rows.astype(jnp.bfloat16).reshape(ROWS, H * HD)
        attention = jnp.dot(head_output_rows, out_weight, preferred_element_type=jnp.float32)
        mixed_rows = (tokens_wide + attention).astype(jnp.bfloat16)
        mixed_wide = mixed_rows.astype(jnp.float32)
        scaled = (mixed_wide * post_gain).astype(jnp.bfloat16)
        row_scale = lax.rsqrt(lax.optimization_barrier(jnp.mean(mixed_wide * mixed_wide, axis=1)) + epsilon)[:, None]
        gate = jnp.dot(scaled, gate_projection_matrix, preferred_element_type=jnp.float32) * row_scale
        up_rows = jnp.dot(scaled, up_weight, preferred_element_type=jnp.float32) * row_scale
        activation = (jax.nn.silu(gate) * up_rows).astype(jnp.bfloat16)
        down_sum = jnp.dot(activation, down_weight, preferred_element_type=jnp.float32)
        outputs.append((mixed_wide + down_sum).astype(jnp.bfloat16))
    return (jnp.stack(outputs), latent_cache, lengths.astype(jnp.int32))
```

```python
import functools

import jax
import jax.numpy as jnp
from jax import lax
from jax.experimental import pallas as pl
from jax.experimental.pallas import tpu as pltpu
from jax.sharding import PartitionSpec as P

D = 7168
KVR = 512
ROPE = 64
HD = 128
STEPS = 2
ROWS_DEV = 8
N = 4
OWN = STEPS * ROWS_DEV
HALF = N * N * OWN
WIDTH = D // N
FF_DEV = 576
CHUNK = 2 * HALF // N
MESH = pl.DeviceIdType.MESH


epsilon = 1e-06


def shifted(block, axis, distance):
    devices = range(lax.axis_size(axis))
    route = [((i - distance) % len(devices), i) for i in devices]
    return lax.ppermute(block, axis, route)


def source_slots(moves_step, groups, per_group):
    group_base = jnp.arange(groups, dtype=jnp.int32) * per_group
    right_slot = group_base + moves_step[:, 0]
    left_slot = group_base + moves_step[:, 1]
    source = jnp.arange(groups * per_group, dtype=jnp.int32)
    source = source.at[right_slot].set(jnp.roll(left_slot, -1))
    source = source.at[left_slot].set(jnp.roll(right_slot, 1))
    return source


def rotate_pairs(rotary, positions):
    half_width = rotary.shape[-1] // 2
    frequencies = 10000.0 ** (-2.0 * jnp.arange(half_width, dtype=jnp.float32) / rotary.shape[-1])
    angles = positions.astype(jnp.float32)[:, None] * frequencies[None, :]
    cosine = jnp.cos(angles)
    sine_part = jnp.sin(angles)
    front_half = rotary[:, :half_width]
    back_half = rotary[:, half_width:]
    return jnp.concatenate(
        [front_half * cosine - back_half * sine_part, back_half * cosine + front_half * sine_part],
        axis=1,
    )


def finish_key(latent, positions):
    content = latent[:, :KVR]
    content = content * lax.rsqrt(jnp.mean(content * content, axis=1, keepdims=True) + epsilon)
    return jnp.concatenate([content, rotate_pairs(latent[:, KVR:], positions)], axis=1).astype(
        jnp.bfloat16
    )


class Place:
    def __init__(self):
        dp = lax.axis_index("dp")
        self.x = lax.axis_index("tp")
        self.y = dp // (2 * N)
        self.z = (dp // 2) % N
        self.c = dp % 2
        self.first = self.c * self.y + (1 - self.c) * self.z
        self.second = self.c * self.z + (1 - self.c) * self.y

    def group(self, y, z, c):
        return y * (2 * N) + z * 2 + c

    def on_first(self, k):
        y = self.c * k + (1 - self.c) * self.y
        z = self.c * self.z + (1 - self.c) * k
        return {"dp": self.group(y, z, self.c), "tp": self.x}

    def on_second(self, k):
        y = self.c * self.y + (1 - self.c) * k
        z = self.c * k + (1 - self.c) * self.z
        return {"dp": self.group(y, z, self.c), "tp": self.x}

    def on_core(self):
        return {"dp": self.group(self.y, self.z, 1 - self.c), "tp": self.x}

    def on_x(self, k):
        return {"dp": self.group(self.y, self.z, self.c), "tp": k}


def send(src, dst, send_sem, recv_sem, device):
    copy = pltpu.make_async_remote_copy(
        src_ref=src,
        dst_ref=dst,
        send_sem=send_sem,
        recv_sem=recv_sem,
        device_id=device,
        device_id_type=MESH,
    )
    copy.start()
    return copy


def reduce_over_groups(here, to_peer, own, sums, parts, peer_rows, rows1, rows2, sems):
    core_sem, sem1, sem2 = sems
    core = pltpu.make_async_remote_copy(
        src_ref=to_peer,
        dst_ref=peer_rows,
        send_sem=core_sem.at[0],
        recv_sem=core_sem.at[1],
        device_id=here.on_core(),
        device_id_type=MESH,
    )
    core.wait()
    copies = []
    for o in (2, 1, 3):
        k = lax.rem(here.first + o, N)
        rows = pl.ds(pl.multiple_of(k * N * OWN, N * OWN), N * OWN)
        sums[k] = (
            own[rows, :].astype(jnp.float32) + peer_rows[rows, :].astype(jnp.float32)
        ).astype(jnp.bfloat16)
        copies.append(
            send(sums.at[k], rows1.at[o - 1], sem1.at[0, o - 1], sem1.at[1, o - 1], here.on_first(k))
        )
    for copy in copies:
        copy.wait()
    rows = pl.ds(pl.multiple_of(here.first * N * OWN, N * OWN), N * OWN)
    total = own[rows, :].astype(jnp.float32) + peer_rows[rows, :].astype(jnp.float32)
    for o in range(N - 1):
        total = total + rows1[o].astype(jnp.float32)
    parts[...] = total.astype(jnp.bfloat16).reshape(parts.shape)
    copies = []
    for o in (2, 1, 3):
        k = lax.rem(here.second + o, N)
        copies.append(
            send(parts.at[k], rows2.at[o - 1], sem2.at[0, o - 1], sem2.at[1, o - 1], here.on_second(k))
        )
    for copy in copies:
        copy.wait()
    total = parts[here.second].astype(jnp.float32)
    for o in range(N - 1):
        total = total + rows2[o].astype(jnp.float32)
    return total


def multiply(lhs, weight, out, first_row, rows):
    tile = 256

    @pl.loop(0, WIDTH // tile)
    def _(i):
        columns = pl.ds(pl.multiple_of(i * tile, tile), tile)
        out[:, columns] = jnp.dot(
            lhs[pl.ds(first_row, rows), :], weight[:, columns], preferred_element_type=jnp.float32
        ).astype(jnp.bfloat16)


def back_kernel(
    heads, tokens, gain, wo_hbm, wg_hbm, wu_hbm, wd_hbm,
    out,
    wo, wg, wu, wd, head_rows, head_block,
    to_peer, own, peer_a, peer_d, sums, parts, rows1_a, rows1_d, rows2_a, rows2_d,
    norms, norm_rows, mixed_all, gate_part, up_part, gate_rows, up_rows, activation,
    weight_sem, head_send, head_recv, core_a, sem1_a, sem2_a, core_d, sem1_d, sem2_d,
    norm_sem, gather2, gather1, gather_core, gate_sem, up_sem, act_sem,
):
    here = Place()
    loads = []
    for i, (src, dst) in enumerate(((wo_hbm, wo), (wg_hbm, wg), (wu_hbm, wu), (wd_hbm, wd))):
        load = pltpu.make_async_copy(src, dst, weight_sem.at[i])
        load.start()
        loads.append(load)

    barrier = pltpu.get_barrier_semaphore()
    pl.semaphore_signal(barrier, inc=1, device_id=here.on_core(), device_id_type=MESH)
    for o in range(1, N):
        for device in (
            here.on_first(lax.rem(here.first + o, N)),
            here.on_second(lax.rem(here.second + o, N)),
            here.on_x(lax.rem(here.x + o, N)),
        ):
            pl.semaphore_signal(barrier, inc=1, device_id=device, device_id_type=MESH)

    me = here.group(here.y, here.z, here.c)

    @pl.loop(0, 2 * N * N)
    def _(i):
        d = lax.rem(me + i, 2 * N * N)

        @pl.when((d != me) | (here.x != here.y))
        def _():
            pl.semaphore_signal(barrier, inc=1, device_id={"dp": d, "tp": here.y}, device_id_type=MESH)

    away = jnp.where(here.x == here.y, 0, 1)
    pl.semaphore_wait(barrier, 1 + 3 * (N - 1) + 2 * N * N - 1 + away)

    place = here.c * (N * N) + here.first * N + here.second
    k_me = here.z * 2 + here.c

    def head_copy(i):
        k = lax.rem(k_me + i // N, 2 * N)
        x = lax.rem(here.x + i, N)
        return k, x, pltpu.make_async_remote_copy(
            src_ref=heads.at[k],
            dst_ref=head_rows.at[place],
            send_sem=head_send.at[i],
            recv_sem=head_recv.at[place],
            device_id={"dp": here.x * (2 * N) + k, "tp": x},
            device_id_type=MESH,
        )

    kept = pltpu.make_async_copy(heads.at[k_me], head_rows.at[place], head_recv.at[place])

    @pl.loop(0, 2 * N * N)
    def _(i):
        k, x, copy = head_copy(i)

        @pl.when((x == here.x) & (k == k_me) & (here.x == here.y))
        def _():
            kept.start()

        @pl.when((x != here.x) | (k != k_me) | (here.x != here.y))
        def _():
            copy.start()

    @pl.loop(0, 2 * N * N)
    def _(i):
        pltpu.make_async_copy(heads.at[0], head_rows.at[i], head_recv.at[i]).wait()

    @pl.loop(0, 2 * N * N)
    def _(i):
        k, x, copy = head_copy(i)

        @pl.when((x != here.x) | (k != k_me) | (here.x != here.y))
        def _():
            copy.wait_send()

    for h in range(N):
        head_block[:, h * HD : (h + 1) * HD] = head_rows[:, h].reshape(2 * HALF, HD)

    other_row = pl.multiple_of((1 - here.c) * HALF, HALF)
    own_row = pl.multiple_of(here.c * HALF, HALF)
    loads[0].wait()
    multiply(head_block, wo, to_peer, other_row, HALF)
    send(to_peer, peer_a, core_a.at[0], core_a.at[1], here.on_core())
    multiply(head_block, wo, own, own_row, HALF)
    attention = reduce_over_groups(
        here, to_peer, own, sums, parts, peer_a, rows1_a, rows2_a, (core_a, sem1_a, sem2_a)
    )
    mixed = (tokens[...].astype(jnp.float32) + attention).astype(jnp.bfloat16).astype(jnp.float32)

    norms[...] = jnp.broadcast_to(jnp.sum(mixed * mixed, axis=1, keepdims=True), norms.shape)
    copies = []
    for o in (2, 1, 3):
        x = lax.rem(here.x + o, N)
        copies.append(
            send(norms, norm_rows.at[o - 1], norm_sem.at[0, o - 1], norm_sem.at[1, o - 1], here.on_x(x))
        )
    for copy in copies:
        copy.wait()
    squares = norms[...]
    for o in range(N - 1):
        squares = squares + norm_rows[o]
    scale = lax.rsqrt(squares / D + epsilon)[:, :1]
    mixed_all[here.c, here.first, here.second] = (mixed * gain[...] * scale).astype(jnp.bfloat16)

    mine = mixed_all.at[here.c, here.first, here.second]
    copies = []
    for o in (2, 1, 3):
        k = lax.rem(here.second + o, N)
        copies.append(send(mine, mine, gather2.at[0, o - 1], gather2.at[1, o - 1], here.on_second(k)))
    for copy in copies:
        copy.wait()
    mine = mixed_all.at[here.c, here.first]
    copies = []
    for o in (2, 1, 3):
        k = lax.rem(here.first + o, N)
        copies.append(send(mine, mine, gather1.at[0, o - 1], gather1.at[1, o - 1], here.on_first(k)))
    handed = [send(mine, mine, gather_core.at[0, 0], gather_core.at[1, 0], here.on_core())]
    for o, copy in zip((2, 1, 3), copies):
        copy.wait()
        block = mixed_all.at[here.c, lax.rem(here.first + N - o, N)]
        handed.append(send(block, block, gather_core.at[0, o], gather_core.at[1, o], here.on_core()))

    loads[1].wait()
    loads[2].wait()

    def chunk_of(i):
        return 2 * lax.rem(here.c + i // 2, 2) + lax.rem(here.x + i, 2)

    def chunk_copies(k):
        o = lax.rem(k - here.x + N, N)
        slot = o - 1
        return [
            pltpu.make_async_remote_copy(
                src_ref=part.at[k],
                dst_ref=rows.at[slot],
                send_sem=sem.at[0, slot],
                recv_sem=sem.at[1, slot],
                device_id=here.on_x(k),
                device_id_type=MESH,
            )
            for part, rows, sem in ((gate_part, gate_rows, gate_sem), (up_part, up_rows, up_sem))
        ]

    for i in range(N):
        if i == 2:
            for copy in handed:
                copy.wait()
        k = chunk_of(i)
        lhs = mixed_all[k // 2, pl.ds(2 * lax.rem(k, 2), 2)].reshape(CHUNK, WIDTH)
        gate_part[k] = jnp.dot(lhs, wg[...], preferred_element_type=jnp.float32).astype(jnp.bfloat16)
        up_part[k] = jnp.dot(lhs, wu[...], preferred_element_type=jnp.float32).astype(jnp.bfloat16)

        @pl.when(k != here.x)
        def _():
            for copy in chunk_copies(k):
                copy.start()

    for o in range(1, N):
        for copy in chunk_copies(lax.rem(here.x + o, N)):
            copy.wait()
    gate = gate_part[here.x].astype(jnp.float32)
    up = up_part[here.x].astype(jnp.float32)
    for o in range(N - 1):
        gate = gate + gate_rows[o].astype(jnp.float32)
        up = up + up_rows[o].astype(jnp.float32)
    activation[here.x] = (gate / (1.0 + jnp.exp(-gate)) * up).astype(jnp.bfloat16)
    mine = activation.at[here.x]
    copies = []
    for o in (2, 1, 3):
        x = lax.rem(here.x + o, N)
        copies.append(send(mine, mine, act_sem.at[0, o - 1], act_sem.at[1, o - 1], here.on_x(x)))
    for copy in copies:
        copy.wait()

    loads[3].wait()
    act_rows = activation.reshape(2 * HALF, FF_DEV)
    multiply(act_rows, wd, to_peer, other_row, HALF)
    send(to_peer, peer_d, core_d.at[0], core_d.at[1], here.on_core())
    multiply(act_rows, wd, own, own_row, HALF)
    down = reduce_over_groups(
        here, to_peer, own, sums, parts, peer_d, rows1_d, rows2_d, (core_d, sem1_d, sem2_d)
    )
    out[...] = (mixed + down).astype(jnp.bfloat16)


def back(heads, tokens, gain, wo, wg, wu, wd):
    bf16, f32 = jnp.bfloat16, jnp.float32
    vmem = pl.BlockSpec(memory_space=pltpu.VMEM)
    hbm = pl.BlockSpec(memory_space=pl.ANY)
    dma = pltpu.SemaphoreType.DMA
    return pl.pallas_call(
        back_kernel,
        out_shape=jax.ShapeDtypeStruct((OWN, WIDTH), bf16),
        in_specs=[vmem, vmem, vmem, hbm, hbm, hbm, hbm],
        out_specs=vmem,
        scratch_shapes=[
            pltpu.VMEM(wo.shape, bf16),
            pltpu.VMEM(wg.shape, bf16),
            pltpu.VMEM(wu.shape, bf16),
            pltpu.VMEM(wd.shape, bf16),
            pltpu.VMEM((2 * N * N, N, OWN, HD), bf16),
            pltpu.VMEM((2 * HALF, N * HD), bf16),
            pltpu.VMEM((HALF, WIDTH), bf16),
            pltpu.VMEM((HALF, WIDTH), bf16),
            pltpu.VMEM((HALF, WIDTH), bf16),
            pltpu.VMEM((HALF, WIDTH), bf16),
            pltpu.VMEM((N, N * OWN, WIDTH), bf16),
            pltpu.VMEM((N, OWN, WIDTH), bf16),
            pltpu.VMEM((N - 1, N * OWN, WIDTH), bf16),
            pltpu.VMEM((N - 1, N * OWN, WIDTH), bf16),
            pltpu.VMEM((N - 1, OWN, WIDTH), bf16),
            pltpu.VMEM((N - 1, OWN, WIDTH), bf16),
            pltpu.VMEM((OWN, 128), f32),
            pltpu.VMEM((N - 1, OWN, 128), f32),
            pltpu.VMEM((2, N, N, OWN, WIDTH), bf16),
            pltpu.VMEM((N, CHUNK, FF_DEV), bf16),
            pltpu.VMEM((N, CHUNK, FF_DEV), bf16),
            pltpu.VMEM((N - 1, CHUNK, FF_DEV), bf16),
            pltpu.VMEM((N - 1, CHUNK, FF_DEV), bf16),
            pltpu.VMEM((N, CHUNK, FF_DEV), bf16),
            dma((4,)),
            dma((2 * N * N,)),
            dma((2 * N * N,)),
            dma((2,)),
            dma((2, N - 1)),
            dma((2, N - 1)),
            dma((2,)),
            dma((2, N - 1)),
            dma((2, N - 1)),
            dma((2, N - 1)),
            dma((2, N - 1)),
            dma((2, N - 1)),
            dma((2, N)),
            dma((2, N - 1)),
            dma((2, N - 1)),
            dma((2, N - 1)),
        ],
        compiler_params=pltpu.CompilerParams(
            collective_id=0, has_side_effects=True, vmem_limit_bytes=56 * 1024 * 1024
        ),
        name="back",
    )(heads, tokens, gain, wo, wg, wu, wd)


def on_device(
    latent_cache,
    lengths,
    slot_moves,
    hidden_in,
    queries,
    latent_weight,
    value_up_projection,
    out_weight,
    post_gain,
    gate_projection_matrix,
    up_weight,
    down_weight,
):
    per_group = latent_cache.shape[0]
    capacity = latent_cache.shape[1]
    groups = lax.axis_size("dp")
    group_position_index = lax.axis_index("dp")
    score_scale = (HD + ROPE) ** (-0.5)
    slot_ids = jnp.arange(per_group, dtype=jnp.int32)
    positions = jnp.arange(capacity, dtype=jnp.int32)
    tokens = hidden_in.reshape(OWN, WIDTH)
    tokens_wide = tokens.astype(jnp.float32)
    partial_latent = jnp.dot(tokens, latent_weight, preferred_element_type=jnp.float32)
    latent_sum, squared_entry_sum = lax.psum(
        (partial_latent, jnp.sum(tokens_wide * tokens_wide, axis=1)), "tp"
    )
    latents = latent_sum * lax.rsqrt(squared_entry_sum / D + epsilon)[:, None]
    heads = []
    for step_index in range(STEPS):
        source = source_slots(slot_moves[step_index], groups, per_group)
        held_lengths = lengths[source]
        own_moves = lax.dynamic_index_in_dim(
            slot_moves[step_index], group_position_index, 0, keepdims=False
        )
        right_out = own_moves[0]
        left_out = own_moves[1]
        leaving_right = lax.dynamic_index_in_dim(latent_cache, right_out, 0, keepdims=False)
        leaving_left = lax.dynamic_index_in_dim(latent_cache, left_out, 0, keepdims=False)
        from_left = shifted(leaving_right, "dp", 1)
        from_right = shifted(leaving_left, "dp", -1)
        latent_cache = lax.dynamic_update_index_in_dim(latent_cache, from_left, left_out, 0)
        latent_cache = lax.dynamic_update_index_in_dim(latent_cache, from_right, right_out, 0)
        own_lengths = lax.dynamic_slice_in_dim(
            held_lengths, group_position_index * per_group, per_group
        )
        latent = latents[step_index * per_group : (step_index + 1) * per_group]
        fresh_key = finish_key(latent, own_lengths)
        latent_cache = latent_cache.at[slot_ids, own_lengths].set(fresh_key)
        lengths = held_lengths + 1
        visible = positions[None, :] < (own_lengths + 1)[:, None]
        scores = (
            jnp.einsum(
                "rhl,rtl->rht",
                queries[step_index],
                latent_cache,
                preferred_element_type=jnp.float32,
            )
            * score_scale
        )
        scores = jnp.where(visible[:, None, :], scores, -1e30)
        peak_score = jnp.max(scores, axis=2, keepdims=True)
        powers = jnp.exp(scores - peak_score)
        weights = (powers / jnp.sum(powers, axis=2, keepdims=True)).astype(jnp.bfloat16)
        per_head_latent_vector = jnp.einsum(
            "rht,rtk->rhk", weights, latent_cache[:, :, :KVR], preferred_element_type=jnp.float32
        ).astype(jnp.bfloat16)
        heads.append(
            jnp.einsum(
                "gfe,feu->fgu",
                per_head_latent_vector,
                value_up_projection,
                preferred_element_type=jnp.float32,
            ).astype(jnp.bfloat16)
        )
    heads = jnp.concatenate(heads, axis=1).reshape(2 * N, N, OWN, HD)
    layer_out = back(
        heads,
        tokens,
        post_gain.reshape(1, WIDTH),
        out_weight,
        gate_projection_matrix,
        up_weight,
        down_weight,
    )
    return (layer_out.reshape(STEPS, per_group, WIDTH), latent_cache, lengths)


def solution(mesh):
    return jax.shard_map(
        on_device,
        mesh=mesh,
        in_specs=(
            P("dp", None, None),
            P(),
            P(),
            P(None, "dp", "tp"),
            P(None, "dp", "tp", None),
            P("tp", None),
            P("tp", None, None),
            P("dp", "tp"),
            P("tp"),
            P("tp", "dp"),
            P("tp", "dp"),
            P("dp", "tp"),
        ),
        out_specs=(P(None, "dp", "tp"), P("dp", None, None), P()),
        check_vma=False,
    )
```

```python
import math
import types

import jax
import jax.numpy as jnp
from jax import lax
from jax.experimental import pallas as pl
from jax.experimental.pallas import tpu as pltpu
from jax.sharding import PartitionSpec as P

D = 7168
KVR = 512
ROPE = 64
HD = 128
STEPS = 2
ROWS_DEV = 8
N = 4
OWN = STEPS * ROWS_DEV
BLOCKS = N * N
HALF = BLOCKS * ROWS_DEV
WIDTH = D // N
COLS = WIDTH // 2
TILE = 2 * ROWS_DEV
FF_DEV = 576
CHUNK = 2 * HALF // N
HEADS = 32
LAT = KVR + ROPE
GROUPS = 2 * N * N
EARLY = 4
NEAR_FIRST = (1, 3, 2)
FAR_FIRST = (2, 1, 3)
MESH = pl.DeviceIdType.MESH


epsilon = 1e-06


def dot_rows(lhs, rhs):
    return lax.dot_general(
        lhs, rhs, (((1,), (1,)), ((), ())), preferred_element_type=jnp.float32
    )


class Place:
    def __init__(self):
        dp = lax.axis_index("dp")
        self.x = lax.axis_index("tp")
        self.y = dp // (2 * N)
        self.z = (dp // 2) % N
        self.c = dp % 2
        self.first = self.c * self.y + (1 - self.c) * self.z
        self.second = self.c * self.z + (1 - self.c) * self.y
        self.me = dp

    def group(self, y, z, c):
        return y * (2 * N) + z * 2 + c

    def on_first(self, k):
        y = self.c * k + (1 - self.c) * self.y
        z = self.c * self.z + (1 - self.c) * k
        return {"dp": self.group(y, z, self.c), "tp": self.x}

    def on_second(self, k):
        y = self.c * self.y + (1 - self.c) * k
        z = self.c * k + (1 - self.c) * self.z
        return {"dp": self.group(y, z, self.c), "tp": self.x}

    def on_core(self):
        return {"dp": self.group(self.y, self.z, 1 - self.c), "tp": self.x}

    def on_x(self, k):
        return {"dp": self.me, "tp": k}

    def on_ring(self, o):
        return {"dp": lax.rem(self.me + o + GROUPS, GROUPS), "tp": self.x}


def remote(src, dst, send_sem, recv_sem, device):
    return pltpu.make_async_remote_copy(
        src_ref=src,
        dst_ref=dst,
        send_sem=send_sem,
        recv_sem=recv_sem,
        device_id=device,
        device_id_type=MESH,
    )


def send(*args):
    copy = remote(*args)
    copy.start()
    return copy


def stacked(rows):
    left = rows[:, :COLS].reshape(-1, ROWS_DEV, COLS)
    right = rows[:, COLS:].reshape(-1, ROWS_DEV, COLS)
    return jnp.concatenate([left, right], axis=1)


def unstacked(blocks):
    left = blocks[:, :ROWS_DEV].reshape(-1, COLS)
    right = blocks[:, ROWS_DEV:].reshape(-1, COLS)
    return jnp.concatenate([left, right], axis=1)


def project(lhs, weight, out):
    for start in range(0, COLS, 256):
        width = min(256, COLS - start)
        parts = [
            jnp.dot(
                lhs, weight[:, first + start : first + start + width], preferred_element_type=jnp.float32
            ).reshape(-1, ROWS_DEV, width)
            for first in (0, COLS)
        ]
        out[:, :, start : start + width] = jnp.concatenate(parts, axis=1).astype(jnp.bfloat16)


def source_of(moves, step, group, slot):
    right = lax.rem(group + 1, GROUPS)
    left = lax.rem(group + GROUPS - 1, GROUPS)
    to_right = slot == moves[step, 0, group]
    to_left = slot == moves[step, 1, group]
    source_group = jnp.where(to_right, right, jnp.where(to_left, left, group))
    source_slot = jnp.where(
        to_right, moves[step, 1, right], jnp.where(to_left, moves[step, 0, left], slot)
    )
    return source_group, source_slot


def held_first(lengths, moves, group, slot):
    source_group, source_slot = source_of(moves, 0, group, slot)
    return lengths[source_group * ROWS_DEV + source_slot]


def held_second(lengths, moves, group, slot):
    source_group, source_slot = source_of(moves, 1, group, slot)
    return held_first(lengths, moves, source_group, source_slot) + 1


def slot_order(moves, group):
    free_before, slots, places = 0, [0] * ROWS_DEV, []
    for j in range(ROWS_DEV):
        moved = (
            (j == moves[0, 0, group])
            | (j == moves[0, 1, group])
            | (j == moves[1, 0, group])
            | (j == moves[1, 1, group])
        )
        early = jnp.where(moved | (free_before >= EARLY), 0, 1)
        place = jnp.where(early == 1, free_before, EARLY + j - free_before)
        places.append(place)
        slots = [jnp.where(place == p, j, slots[p]) for p in range(ROWS_DEV)]
        free_before = free_before + early
    return slots, places


def with_row(block, position, row):
    rows = lax.broadcasted_iota(jnp.int32, block.shape, 0)
    return jnp.where(rows == position, jnp.broadcast_to(row, block.shape), block)


def attend(query_rows, keys, live):
    scores = dot_rows(query_rows, keys[...]) * (HD + ROPE) ** (-0.5)
    positions = lax.broadcasted_iota(jnp.int32, scores.shape, 1)
    scores = jnp.where(positions < live, scores, -1e30)
    powers = jnp.exp(scores - jnp.max(scores, axis=1, keepdims=True))
    weights = (powers / jnp.sum(powers, axis=1, keepdims=True)).astype(jnp.bfloat16)
    return jnp.dot(weights, keys[:, :KVR], preferred_element_type=jnp.float32)


def fresh_keys(latent, positions):
    content = latent[:, :KVR]
    content = content * lax.rsqrt(jnp.mean(content * content, axis=1, keepdims=True) + epsilon)
    rotary = latent[:, KVR:]
    lane = lax.broadcasted_iota(jnp.int32, rotary.shape, 1)
    half = ROPE // 2
    power = lax.rem(lane, half).astype(jnp.float32) * (-2.0 / ROPE * math.log(10000.0))
    angles = positions.astype(jnp.float32) * jnp.exp(power)
    turned = jnp.where(lane < half, -pltpu.roll(rotary, 128 - half, 1), pltpu.roll(rotary, half, 1))
    return content, rotary * jnp.cos(angles) + turned * jnp.sin(angles)


def enter(here, barrier):
    devices = [here.on_ring(1), here.on_ring(-1), here.on_core()]
    for o in range(1, N):
        devices.append(here.on_x(lax.rem(here.x + o, N)))
        devices.append(here.on_first(lax.rem(here.first + o, N)))
        devices.append(here.on_second(lax.rem(here.second + o, N)))
    for device in devices:
        pl.semaphore_signal(barrier, inc=1, device_id=device, device_id_type=MESH)

    @pl.loop(0, GROUPS)
    def _(i):
        d = lax.rem(here.me + i, GROUPS)

        @pl.when((d != here.me) | (here.x != here.y))
        def _():
            pl.semaphore_signal(barrier, inc=1, device_id={"dp": d, "tp": here.y}, device_id_type=MESH)

    return len(devices) + GROUPS - 1 + jnp.where(here.x == here.y, 0, 1)


def head_copy(here, r, step, i):
    place = here.c * BLOCKS + here.first * N + here.second
    k = lax.rem(here.z * 2 + here.c + i // N, 2 * N)
    x = lax.rem(here.x + i, N)
    kept = (x == here.x) & (here.x * (2 * N) + k == here.me)

    def copy():
        return remote(
            r.heads.at[step, k],
            r.head_rows.at[step, place],
            r.head_send.at[step, i],
            r.head_recv.at[step, place],
            {"dp": here.x * (2 * N) + k, "tp": x},
        )

    def local():
        return pltpu.make_async_copy(
            r.heads.at[step, k], r.head_rows.at[step, place], r.head_recv.at[step, place]
        )

    return kept, copy, local


def value_up(here, r, step, places):
    for j in range(ROWS_DEV):
        block = r.head_latent[step * ROWS_DEV + places[j]]
        for c in range(KVR // 128):
            r.head_sorted[c, j * HEADS : (j + 1) * HEADS, :] = block[:, c * 128 : (c + 1) * 128]

    def head(h):
        rows = jnp.concatenate(
            [r.head_sorted.at[c][pl.ds(h, ROWS_DEV, stride=HEADS), :] for c in range(KVR // 128)], axis=1
        ).astype(jnp.bfloat16)
        return jnp.dot(rows, r.vup[h], preferred_element_type=jnp.float32)

    for h in range(0, HEADS, 2):
        r.heads[step, h // N, h % N // 2] = jnp.concatenate([head(h), head(h + 1)], axis=0).astype(jnp.bfloat16)

    @pl.loop(0, GROUPS)
    def _(i):
        kept, copy, local = head_copy(here, r, step, i)

        @pl.when(kept)
        def _():
            local().start()

        @pl.when(jnp.logical_not(kept))
        def _():
            copy().start()


def front_line(here, r):
    loads = []
    for i, (src, dst) in enumerate(
        (
            (r.cache_hbm, r.cache),
            (r.lw_hbm, r.lw),
            (r.queries_hbm, r.queries),
            (r.vup_hbm, r.vup),
            (r.wo_hbm, r.wo),
            (r.wg_hbm, r.wg),
            (r.wu_hbm, r.wu),
            (r.wd_hbm, r.wd),
        )
    ):
        load = pltpu.make_async_copy(src, dst, r.load_sem.at[i])
        load.start()
        loads.append(load)
    r.weight_loads = loads[4:]
    barrier = pltpu.get_barrier_semaphore()
    entered = enter(here, barrier)

    moves, me = r.moves, here.me
    a0, b0, a1, b1 = moves[0, 0, me], moves[0, 1, me], moves[1, 0, me], moves[1, 1, me]
    slots, places = slot_order(moves, me)

    loads[0].wait()
    r.leaving0[0] = r.cache[a0]
    r.leaving0[1] = r.cache[b0]
    pl.semaphore_wait(barrier, entered)
    moving0 = [
        send(r.leaving0.at[i], r.arrived0.at[i], r.move0_sem.at[0, i], r.move0_sem.at[1, i], here.on_ring(o))
        for i, o in enumerate((1, -1))
    ]

    loads[1].wait()
    wide = r.tokens[...].astype(jnp.float32)
    r.latents[...] = jnp.zeros_like(r.latents)
    r.latents[:, :LAT] = dot_rows(r.tokens[...], r.lw[...])
    r.latents[:, LAT + 64 :] = jnp.broadcast_to(jnp.sum(wide * wide, axis=1, keepdims=True), (OWN, 128))
    copies = [
        send(
            r.latents,
            r.latent_rows.at[o - 1],
            r.latent_sem.at[0, o - 1],
            r.latent_sem.at[1, o - 1],
            here.on_x(lax.rem(here.x + o, N)),
        )
        for o in FAR_FIRST
    ]
    held = [held_first(r.lengths, moves, me, j) for j in range(ROWS_DEV)]
    held += [held_second(r.lengths, moves, me, j) for j in range(ROWS_DEV)]
    row = lax.broadcasted_iota(jnp.int32, (OWN, 128), 0)
    positions = jnp.zeros((OWN, 128), jnp.int32)
    for i in range(OWN):
        positions = jnp.where(row == i, held[i], positions)

    def held_at(step, place):
        result = held[step * ROWS_DEV]
        for j in range(1, ROWS_DEV):
            result = jnp.where(slots[place] == j, held[step * ROWS_DEV + j], result)
        return result

    yield
    for copy in copies:
        copy.wait()
    total = r.latents[...]
    for o in range(N - 1):
        total = total + r.latent_rows[o]
    scale = lax.rsqrt(total[:, LAT + 64 :] / D + epsilon)[:, :1]
    content, rotary = fresh_keys(total[:, : LAT + 64] * scale, positions)
    r.fresh[:, :KVR] = content
    r.fresh[:, KVR:] = rotary

    def fresh_row(step, place):
        return r.fresh[pl.ds(step * ROWS_DEV + slots[place], 1), :LAT].astype(jnp.bfloat16)

    loads[2].wait()
    r.ordered_copies = []
    for p in range(EARLY):
        first, second = held_at(0, p), held_at(1, p)
        block = with_row(r.cache[slots[p]], first, fresh_row(0, p))
        r.early_keys[p] = with_row(block, second, fresh_row(1, p))
        copy = pltpu.make_async_copy(r.early_keys.at[p], r.ordered.at[p], r.out_sem.at[p])
        copy.start()
        r.ordered_copies.append(copy)
        rows = jnp.concatenate([r.queries[0, slots[p]], r.queries[1, slots[p]]], axis=0)
        step_row = lax.broadcasted_iota(jnp.int32, (2 * HEADS, 1), 0)
        live = jnp.where(step_row < HEADS, first + 1, second + 1)
        result = attend(rows, r.early_keys.at[p], live)
        r.head_latent[p] = result[:HEADS]
        r.head_latent[ROWS_DEV + p] = result[HEADS:]

    yield
    for copy in moving0:
        copy.wait()
    for p in range(EARLY, ROWS_DEV):
        block = jnp.where(
            slots[p] == a0, r.arrived0[1], jnp.where(slots[p] == b0, r.arrived0[0], r.cache[slots[p]])
        )
        r.keys0[p - EARLY] = with_row(block, held_at(0, p), fresh_row(0, p))
    place_a, place_b = 0, 0
    for p in range(EARLY, ROWS_DEV):
        place_a = jnp.where(slots[p] == a1, p - EARLY, place_a)
        place_b = jnp.where(slots[p] == b1, p - EARLY, place_b)
    r.leaving1[0] = r.keys0[place_a]
    r.leaving1[1] = r.keys0[place_b]
    moving1 = [
        send(r.leaving1.at[i], r.arrived1.at[i], r.move1_sem.at[0, i], r.move1_sem.at[1, i], here.on_ring(o))
        for i, o in enumerate((1, -1))
    ]
    for p in range(EARLY, ROWS_DEV):
        r.head_latent[p] = attend(r.queries[0, slots[p]], r.keys0.at[p - EARLY], held_at(0, p) + 1)
    loads[3].wait()
    value_up(here, r, 0, places)

    yield
    for copy in moving1:
        copy.wait()
    for p in range(EARLY, ROWS_DEV):
        block = jnp.where(
            slots[p] == a1, r.arrived1[1], jnp.where(slots[p] == b1, r.arrived1[0], r.keys0[p - EARLY])
        )
        r.keys1[p - EARLY] = with_row(block, held_at(1, p), fresh_row(1, p))
        copy = pltpu.make_async_copy(r.keys1.at[p - EARLY], r.ordered.at[p], r.out_sem.at[p])
        copy.start()
        r.ordered_copies.append(copy)
    for p in range(EARLY, ROWS_DEV):
        r.head_latent[ROWS_DEV + p] = attend(
            r.queries[1, slots[p]], r.keys1.at[p - EARLY], held_at(1, p) + 1
        )
    yield
    value_up(here, r, 1, places)
    yield


def reduce_over_groups(here, r, step, use):
    own, peer = r.own.at[step], r.peer_rows.at[use, step]
    core_sem, sem1, sem2 = r.core_sem.at[use, step], r.sem1.at[use, step], r.sem2.at[use, step]
    sums, parts, rows1, rows2 = r.sums.at[step], r.parts.at[step], r.rows1.at[use, step], r.rows2.at[use, step]
    remote(r.to_peer.at[step], peer, core_sem.at[0], core_sem.at[1], here.on_core()).wait()

    def both(k):
        blocks = pl.ds(k * N, N)
        return own[blocks].astype(jnp.float32) + peer[blocks].astype(jnp.float32)

    copies = {}
    for o in FAR_FIRST:
        k = lax.rem(here.first + o, N)
        sums[k] = both(k).astype(jnp.bfloat16)
        copies[o] = send(sums.at[k], rows1.at[o - 1], sem1.at[0, o - 1], sem1.at[1, o - 1], here.on_first(k))
    total = both(here.first)
    yield
    for o in NEAR_FIRST:
        copies[o].wait()
        total = total + rows1[o - 1].astype(jnp.float32)
    parts[...] = total.astype(jnp.bfloat16)
    copies = {}
    for o in FAR_FIRST:
        k = lax.rem(here.second + o, N)
        copies[o] = send(parts.at[k], rows2.at[o - 1], sem2.at[0, o - 1], sem2.at[1, o - 1], here.on_second(k))
    yield
    total = parts[here.second].astype(jnp.float32)
    for o in NEAR_FIRST:
        copies[o].wait()
        total = total + rows2[o - 1].astype(jnp.float32)
    return total


def project_both(here, r, step, use, lhs, weight):
    project(lhs(1 - here.c), weight, r.to_peer.at[step])
    core_sem = r.core_sem.at[use, step]
    send(r.to_peer.at[step], r.peer_rows.at[use, step], core_sem.at[0], core_sem.at[1], here.on_core())
    project(lhs(here.c), weight, r.own.at[step])


def back_line(here, r, step):
    f32, bf16 = jnp.float32, jnp.bfloat16

    @pl.loop(0, GROUPS)
    def _(i):
        pltpu.make_async_copy(r.heads.at[step, 0], r.head_rows.at[step, i], r.head_recv.at[step, i]).wait()

    @pl.loop(0, GROUPS)
    def _(i):
        kept, copy, _ = head_copy(here, r, step, i)

        @pl.when(jnp.logical_not(kept))
        def _():
            copy().wait_send()

    rows = r.head_rows[step].astype(f32)
    for h in range(N):
        first = h % 2 * ROWS_DEV
        r.head_block[:, h * HD : (h + 1) * HD] = (
            rows[:, h // 2, first : first + ROWS_DEV].reshape(2 * HALF, HD).astype(bf16)
        )
    if step == 0:
        r.weight_loads[0].wait()

    def half(ref, c):
        return ref[pl.ds(pl.multiple_of(c * HALF, HALF), HALF), :]

    project_both(here, r, step, 0, lambda c: half(r.head_block, c), r.wo[...])
    yield
    attention = yield from reduce_over_groups(here, r, step, 0)
    tokens = stacked(r.tokens[...].astype(f32)[step * ROWS_DEV : (step + 1) * ROWS_DEV])[0]
    mixed = (tokens + attention).astype(bf16).astype(f32)
    r.mixed[step] = mixed

    squares = jnp.sum(mixed * mixed, axis=1, keepdims=True)
    squares = squares[:ROWS_DEV] + squares[ROWS_DEV:]
    norms, norm_rows, sem = r.norms.at[step], r.norm_rows.at[step], r.norm_sem.at[step]
    norms[...] = jnp.broadcast_to(squares, norms.shape)
    copies = {}
    for o in FAR_FIRST:
        x = lax.rem(here.x + o, N)
        copies[o] = send(norms, norm_rows.at[o - 1], sem.at[0, o - 1], sem.at[1, o - 1], here.on_x(x))
    yield
    squares = norms[...]
    for o in NEAR_FIRST:
        copies[o].wait()
        squares = squares + norm_rows[o - 1]
    scale = lax.rsqrt(squares / D + epsilon)[:, :1]
    scale = jnp.concatenate([scale, scale], axis=0)
    gain = stacked(jnp.broadcast_to(r.gain[...].reshape(1, WIDTH), (ROWS_DEV, WIDTH)))[0]
    mixed_all = r.mixed_all.at[step]
    mixed_all[here.c, here.first, here.second] = (r.mixed[step] * gain * scale).astype(bf16)

    mine = mixed_all.at[here.c, here.first, here.second]
    sem = r.gather2.at[step]
    copies = {}
    for o in FAR_FIRST:
        k = lax.rem(here.second + o, N)
        copies[o] = send(mine, mine, sem.at[0, o - 1], sem.at[1, o - 1], here.on_second(k))
    yield
    for o in NEAR_FIRST:
        copies[o].wait()
    mine = mixed_all.at[here.c, here.first]
    sem, core_sem = r.gather1.at[step], r.gather_core.at[step]
    copies = {}
    for o in FAR_FIRST:
        k = lax.rem(here.first + o, N)
        copies[o] = send(mine, mine, sem.at[0, o - 1], sem.at[1, o - 1], here.on_first(k))
    handed = [send(mine, mine, core_sem.at[0, 0], core_sem.at[1, 0], here.on_core())]
    yield
    for o in NEAR_FIRST:
        copies[o].wait()
        block = mixed_all.at[here.c, lax.rem(here.first + N - o, N)]
        handed.append(send(block, block, core_sem.at[0, o], core_sem.at[1, o], here.on_core()))

    if step == 0:
        r.weight_loads[1].wait()
        r.weight_loads[2].wait()
    sums = (
        (r.gate_part.at[step], r.gate_rows.at[step], r.gate_sem.at[step], r.wg),
        (r.up_part.at[step], r.up_rows.at[step], r.up_sem.at[step], r.wu),
    )

    def chunk_copy(part, rows, sem, k):
        slot = lax.rem(k - here.x + N, N) - 1
        return remote(part.at[k], rows.at[slot], sem.at[0, slot], sem.at[1, slot], here.on_x(k))

    for core in (here.c, 1 - here.c):
        if core is not here.c:
            yield
            for copy in handed:
                copy.wait()
        r.lhs[...] = unstacked(mixed_all[core].astype(f32).reshape(BLOCKS, TILE, COLS)).astype(bf16)
        for part, rows, sem, weight in sums:
            part[pl.ds(2 * core, 2)] = dot_rows(r.lhs[...], weight[...]).astype(bf16).reshape(2, CHUNK, FF_DEV)
            for i in range(2):
                k = 2 * core + lax.rem(here.x + i, 2)

                @pl.when(k != here.x)
                def _():
                    chunk_copy(part, rows, sem, k).start()

    yield
    totals = []
    for part, rows, sem, _ in sums:
        total = part[here.x].astype(f32)
        for o in NEAR_FIRST:
            chunk_copy(part, rows, sem, lax.rem(here.x + o, N)).wait()
        for o in range(N - 1):
            total = total + rows[o].astype(f32)
        totals.append(total)
    gate, up = totals
    activation = r.activation.at[step]
    activation[here.x] = (gate / (1.0 + jnp.exp(-gate)) * up).astype(bf16)
    mine = activation.at[here.x]
    sem = r.act_sem.at[step]
    copies = {}
    for o in FAR_FIRST:
        x = lax.rem(here.x + o, N)
        copies[o] = send(mine, mine, sem.at[0, o - 1], sem.at[1, o - 1], here.on_x(x))
    yield
    for o in NEAR_FIRST:
        copies[o].wait()

    if step == 0:
        r.weight_loads[3].wait()
    project_both(
        here, r, step, 1, lambda c: activation[pl.ds(2 * c, 2)].reshape(HALF, FF_DEV), r.wd[...]
    )
    yield
    down = yield from reduce_over_groups(here, r, step, 1)
    r.results[step] = unstacked((r.mixed[step] + down)[None])
    yield


ORDER = "FFFF0F001010101010101010101010111"

INPUTS = (
    "lengths", "moves", "tokens", "gain", "lw_hbm", "queries_hbm", "cache_hbm", "vup_hbm",
    "wo_hbm", "wg_hbm", "wu_hbm", "wd_hbm",
)


def layer_kernel(names, *refs):
    r = types.SimpleNamespace(**dict(zip(names, refs)))
    here = Place()
    lines = {"F": front_line(here, r), "0": back_line(here, r, 0), "1": back_line(here, r, 1)}
    for name in ORDER:
        next(lines[name], None)
    r.out[...] = jnp.concatenate([r.results[0], r.results[1]], axis=0).astype(jnp.bfloat16)
    for copy in r.ordered_copies:
        copy.wait()


def layer(lengths, moves, tokens, gain, lw, queries, cache, vup, wo, wg, wu, wd):
    bf16, f32 = jnp.bfloat16, jnp.float32
    vmem = pl.BlockSpec(memory_space=pltpu.VMEM)
    smem = pl.BlockSpec(memory_space=pltpu.SMEM)
    hbm = pl.BlockSpec(memory_space=pl.ANY)
    slot = cache.shape[1:]

    def dma(*shape):
        return pltpu.SemaphoreType.DMA(shape)

    def held(*shape, dtype=bf16):
        return pltpu.VMEM(shape, dtype)

    scratch = dict(
        cache=held(*cache.shape),
        lw=held(*lw.shape),
        queries=held(*queries.shape),
        vup=held(*vup.shape),
        wo=held(*wo.shape),
        wg=held(*wg.shape),
        wu=held(*wu.shape),
        wd=held(*wd.shape),
        latents=held(OWN, LAT + 64 + 128, dtype=f32),
        latent_rows=held(N - 1, OWN, LAT + 64 + 128, dtype=f32),
        fresh=held(OWN, LAT + 64, dtype=f32),
        leaving0=held(2, *slot),
        leaving1=held(2, *slot),
        arrived0=held(2, *slot),
        arrived1=held(2, *slot),
        early_keys=held(EARLY, *slot),
        keys0=held(ROWS_DEV - EARLY, *slot),
        keys1=held(ROWS_DEV - EARLY, *slot),
        head_latent=held(OWN, HEADS, KVR, dtype=f32),
        head_sorted=held(KVR // 128, ROWS_DEV * HEADS, 128, dtype=f32),
        heads=held(STEPS, 2 * N, N // 2, TILE, HD),
        head_rows=held(STEPS, GROUPS, N // 2, TILE, HD),
        head_block=held(2 * HALF, N * HD),
        to_peer=held(STEPS, BLOCKS, TILE, COLS),
        own=held(STEPS, BLOCKS, TILE, COLS),
        peer_rows=held(2, STEPS, BLOCKS, TILE, COLS),
        sums=held(STEPS, N, N, TILE, COLS),
        parts=held(STEPS, N, TILE, COLS),
        rows1=held(2, STEPS, N - 1, N, TILE, COLS),
        rows2=held(2, STEPS, N - 1, TILE, COLS),
        mixed=held(STEPS, TILE, COLS, dtype=f32),
        norms=held(STEPS, ROWS_DEV, 128, dtype=f32),
        norm_rows=held(STEPS, N - 1, ROWS_DEV, 128, dtype=f32),
        mixed_all=held(STEPS, 2, N, N, TILE, COLS),
        lhs=held(HALF, WIDTH),
        gate_part=held(STEPS, N, CHUNK, FF_DEV),
        up_part=held(STEPS, N, CHUNK, FF_DEV),
        gate_rows=held(STEPS, N - 1, CHUNK, FF_DEV),
        up_rows=held(STEPS, N - 1, CHUNK, FF_DEV),
        activation=held(STEPS, N, CHUNK, FF_DEV),
        results=held(STEPS, ROWS_DEV, WIDTH, dtype=f32),
        load_sem=dma(8),
        latent_sem=dma(2, N - 1),
        move0_sem=dma(2, 2),
        move1_sem=dma(2, 2),
        out_sem=dma(ROWS_DEV),
        head_send=dma(STEPS, GROUPS),
        head_recv=dma(STEPS, GROUPS),
        core_sem=dma(2, STEPS, 2),
        sem1=dma(2, STEPS, 2, N - 1),
        sem2=dma(2, STEPS, 2, N - 1),
        norm_sem=dma(STEPS, 2, N - 1),
        gather2=dma(STEPS, 2, N - 1),
        gather1=dma(STEPS, 2, N - 1),
        gather_core=dma(STEPS, 2, N),
        gate_sem=dma(STEPS, 2, N - 1),
        up_sem=dma(STEPS, 2, N - 1),
        act_sem=dma(STEPS, 2, N - 1),
    )
    names = (*INPUTS, "out", "ordered", *scratch)

    def kernel(*refs):
        layer_kernel(names, *refs)

    return pl.pallas_call(
        kernel,
        out_shape=(
            jax.ShapeDtypeStruct((OWN, WIDTH), bf16),
            jax.ShapeDtypeStruct(cache.shape, bf16),
        ),
        in_specs=[smem, smem, vmem, vmem] + [hbm] * 8,
        out_specs=(vmem, hbm),
        scratch_shapes=list(scratch.values()),
        compiler_params=pltpu.CompilerParams(
            collective_id=0, has_side_effects=True, vmem_limit_bytes=58 * 1024 * 1024
        ),
        name="layer",
    )(lengths, moves, tokens, gain, lw, queries, cache, vup, wo, wg, wu, wd)


def finish_kernel(
    lengths, moves, group, ordered, rows, final_cache, final_rows, final_lengths, moved, slots, row_block, sems, row_sem
):
    _, places = slot_order(moves, group[0])
    loads = [pltpu.make_async_copy(ordered.at[places[j]], slots.at[j], sems.at[0, j]) for j in range(ROWS_DEV)]
    stores = [pltpu.make_async_copy(slots.at[j], final_cache.at[j], sems.at[1, j]) for j in range(ROWS_DEV)]
    loads.append(pltpu.make_async_copy(rows, row_block, row_sem.at[0]))
    stores.append(pltpu.make_async_copy(row_block, final_rows, row_sem.at[1]))
    for load in loads:
        load.start()
    for load, store in zip(loads, stores):
        load.wait()
        store.start()

    @pl.loop(0, GROUPS)
    def _(g):
        for j in range(ROWS_DEV):
            moved[g * ROWS_DEV + j] = lengths[g * ROWS_DEV + j] + 1

    @pl.loop(0, GROUPS)
    def _(g):
        right = lax.rem(g + 1, GROUPS)
        left = lax.rem(g + GROUPS - 1, GROUPS)
        moved[g * ROWS_DEV + moves[0, 0, g]] = lengths[right * ROWS_DEV + moves[0, 1, right]] + 1
        moved[g * ROWS_DEV + moves[0, 1, g]] = lengths[left * ROWS_DEV + moves[0, 0, left]] + 1

    @pl.loop(0, GROUPS)
    def _(g):
        for j in range(ROWS_DEV):
            final_lengths[g * ROWS_DEV + j] = moved[g * ROWS_DEV + j] + 1

    @pl.loop(0, GROUPS)
    def _(g):
        right = lax.rem(g + 1, GROUPS)
        left = lax.rem(g + GROUPS - 1, GROUPS)
        final_lengths[g * ROWS_DEV + moves[1, 0, g]] = moved[right * ROWS_DEV + moves[1, 1, right]] + 1
        final_lengths[g * ROWS_DEV + moves[1, 1, g]] = moved[left * ROWS_DEV + moves[1, 0, left]] + 1

    for store in stores:
        store.wait()


def finish(lengths, moves, group, ordered, rows):
    smem = pl.BlockSpec(memory_space=pltpu.SMEM)
    hbm = pl.BlockSpec(memory_space=pltpu.HBM)
    return pl.pallas_call(
        finish_kernel,
        out_shape=(
            jax.ShapeDtypeStruct(ordered.shape, ordered.dtype),
            jax.ShapeDtypeStruct(rows.shape, rows.dtype),
            jax.ShapeDtypeStruct(lengths.shape, jnp.int32),
        ),
        in_specs=[smem, smem, smem, hbm, hbm],
        out_specs=(hbm, hbm, smem),
        scratch_shapes=[
            pltpu.SMEM(lengths.shape, jnp.int32),
            pltpu.VMEM(ordered.shape, ordered.dtype),
            pltpu.VMEM(rows.shape, rows.dtype),
            pltpu.SemaphoreType.DMA((2, ROWS_DEV)),
            pltpu.SemaphoreType.DMA((2,)),
        ],
        compiler_params=pltpu.CompilerParams(vmem_limit_bytes=16 * 1024 * 1024),
        name="finish",
    )(lengths, moves, group, ordered, rows)


def on_device(
    latent_cache,
    lengths,
    slot_moves,
    hidden_in,
    queries,
    latent_weight,
    value_up_projection,
    out_weight,
    post_gain,
    gate_projection_matrix,
    up_weight,
    down_weight,
):
    moves = jnp.swapaxes(slot_moves, 1, 2)
    rows, ordered = layer(
        lengths,
        moves,
        hidden_in.reshape(OWN, WIDTH),
        post_gain,
        latent_weight.T,
        queries,
        latent_cache,
        value_up_projection,
        out_weight,
        gate_projection_matrix.T,
        up_weight.T,
        down_weight,
    )
    group = lax.axis_index("dp").reshape(1)
    final_cache, final_rows, final_lengths = finish(lengths, moves, group, ordered, rows)
    return (final_rows.reshape(STEPS, ROWS_DEV, WIDTH), final_cache, final_lengths)


def solution(mesh):
    return jax.shard_map(
        on_device,
        mesh=mesh,
        in_specs=(
            P("dp", None, None),
            P(),
            P(),
            P(None, "dp", "tp"),
            P(None, "dp", "tp", None),
            P("tp", None),
            P("tp", None, None),
            P("dp", "tp"),
            P("tp"),
            P("tp", "dp"),
            P("tp", "dp"),
            P("dp", "tp"),
        ),
        out_specs=(P(None, "dp", "tp"), P("dp", None, None), P()),
        check_vma=False,
    )
```

```python
import math
import types

import jax
import jax.numpy as jnp
from jax import lax
from jax.experimental import pallas as pl
from jax.experimental.pallas import tpu as pltpu
from jax.sharding import PartitionSpec as P

D = 7168
KVR = 512
ROPE = 64
HD = 128
STEPS = 2
ROWS_DEV = 8
N = 4
OWN = STEPS * ROWS_DEV
BLOCKS = N * N
HALF = BLOCKS * ROWS_DEV
WIDTH = D // N
COLS = WIDTH // 2
TILE = 2 * ROWS_DEV
FF_DEV = 576
CHUNK = 2 * HALF // N
HEADS = 32
LAT = KVR + ROPE
GROUPS = 2 * N * N
EARLY = 4
CAP = 448
MOVE_PARTS = 4
MOVE_ROWS = CAP // MOVE_PARTS
NEAR_FIRST = (1, 3, 2)
FAR_FIRST = (2, 1, 3)
HOPS = (0, 1, 2, 1)
CHIPS = sorted(range(1, N * N), key=lambda o: HOPS[o // N] + HOPS[o % N])
SPARE = 64
MESH = pl.DeviceIdType.MESH


epsilon = 1e-06


def dot_rows(lhs, rhs):
    return lax.dot_general(
        lhs, rhs, (((1,), (1,)), ((), ())), preferred_element_type=jnp.float32
    )


class Place:
    def __init__(self):
        dp = lax.axis_index("dp")
        self.x = lax.axis_index("tp")
        self.y = dp // (2 * N)
        self.z = (dp // 2) % N
        self.c = dp % 2
        self.me = dp

    def on_chip(self, y, z):
        return {"dp": y * (2 * N) + z * 2 + self.c, "tp": self.x}

    def on_core(self):
        return {"dp": self.me + 1 - 2 * self.c, "tp": self.x}

    def on_x(self, k):
        return {"dp": self.me, "tp": k}

    def on_ring(self, o):
        return {"dp": lax.rem(self.me + o + GROUPS, GROUPS), "tp": self.x}

    def chip(self, offset):
        return lax.rem(self.y + offset // N, N), lax.rem(self.z + offset % N, N)


def remote(src, dst, send_sem, recv_sem, device):
    return pltpu.make_async_remote_copy(
        src_ref=src,
        dst_ref=dst,
        send_sem=send_sem,
        recv_sem=recv_sem,
        device_id=device,
        device_id_type=MESH,
    )


def send(*args):
    copy = remote(*args)
    copy.start()
    return copy


def stacked(rows):
    left = rows[:, :COLS].reshape(-1, ROWS_DEV, COLS)
    right = rows[:, COLS:].reshape(-1, ROWS_DEV, COLS)
    return jnp.concatenate([left, right], axis=1)


def unstacked(blocks):
    left = blocks[:, :ROWS_DEV].reshape(-1, COLS)
    right = blocks[:, ROWS_DEV:].reshape(-1, COLS)
    return jnp.concatenate([left, right], axis=1)


def project(lhs, weight, out):
    for start in range(0, COLS, 256):
        width = min(256, COLS - start)
        parts = [
            jnp.dot(
                lhs, weight[:, first + start : first + start + width], preferred_element_type=jnp.float32
            ).reshape(-1, ROWS_DEV, width)
            for first in (0, COLS)
        ]
        out[:, :, start : start + width] = jnp.concatenate(parts, axis=1).astype(jnp.bfloat16)


def in_pieces(value):
    pieces = []
    for _ in range(3):
        piece = value.astype(jnp.bfloat16).astype(jnp.float32)
        pieces.append(piece)
        value = value - piece
    return pieces


def source_of(moves, step, group, slot):
    right = lax.rem(group + 1, GROUPS)
    left = lax.rem(group + GROUPS - 1, GROUPS)
    to_right = slot == moves[step, 0, group]
    to_left = slot == moves[step, 1, group]
    source_group = jnp.where(to_right, right, jnp.where(to_left, left, group))
    source_slot = jnp.where(
        to_right, moves[step, 1, right], jnp.where(to_left, moves[step, 0, left], slot)
    )
    return source_group, source_slot


def held_first(lengths, moves, group, slot):
    source_group, source_slot = source_of(moves, 0, group, slot)
    return lengths[source_group * ROWS_DEV + source_slot]


def held_second(lengths, moves, group, slot):
    source_group, source_slot = source_of(moves, 1, group, slot)
    return held_first(lengths, moves, source_group, source_slot) + 1


def slot_order(moves, group):
    free_before, slots, places = 0, [0] * ROWS_DEV, []
    for j in range(ROWS_DEV):
        moved = (
            (j == moves[0, 0, group])
            | (j == moves[0, 1, group])
            | (j == moves[1, 0, group])
            | (j == moves[1, 1, group])
        )
        early = jnp.where(moved | (free_before >= EARLY), 0, 1)
        place = jnp.where(early == 1, free_before, EARLY + j - free_before)
        places.append(place)
        slots = [jnp.where(place == p, j, slots[p]) for p in range(ROWS_DEV)]
        free_before = free_before + early
    return slots, places


def with_row(block, position, row):
    rows = lax.broadcasted_iota(jnp.int32, block.shape, 0)
    return jnp.where(rows == position, jnp.broadcast_to(row, block.shape), block)


def attend(query_rows, keys, live):
    scores = dot_rows(query_rows, keys[...]) * (HD + ROPE) ** (-0.5)
    positions = lax.broadcasted_iota(jnp.int32, scores.shape, 1)
    scores = jnp.where(positions < live, scores, -1e30)
    powers = jnp.exp(scores - jnp.max(scores, axis=1, keepdims=True))
    weights = (powers / jnp.sum(powers, axis=1, keepdims=True)).astype(jnp.bfloat16)
    return jnp.dot(weights, keys[:, :KVR], preferred_element_type=jnp.float32)


def fresh_keys(latent, positions):
    content = latent[:, :KVR]
    content = content * lax.rsqrt(jnp.mean(content * content, axis=1, keepdims=True) + epsilon)
    rotary = latent[:, KVR:]
    lane = lax.broadcasted_iota(jnp.int32, rotary.shape, 1)
    half = ROPE // 2
    power = lax.rem(lane, half).astype(jnp.float32) * (-2.0 / ROPE * math.log(10000.0))
    angles = positions.astype(jnp.float32) * jnp.exp(power)
    turned = jnp.where(lane < half, -pltpu.roll(rotary, 128 - half, 1), pltpu.roll(rotary, half, 1))
    return content, rotary * jnp.cos(angles) + turned * jnp.sin(angles)


def enter(here, barrier):
    devices = [here.on_ring(1), here.on_ring(-1), here.on_core()]
    for o in range(1, N):
        devices += [here.on_x(lax.rem(here.x + o, N)), here.on_chip(*here.chip(o)), here.on_chip(*here.chip(o * N))]
    for device in devices:
        pl.semaphore_signal(barrier, inc=1, device_id=device, device_id_type=MESH)
    return len(devices)


def tell(here, sem, line):
    for device in known_line(here, line):
        pl.semaphore_signal(sem, inc=1, device_id=device, device_id_type=MESH)


def hear(here, sem, line):
    pl.semaphore_wait(sem, len(known_line(here, line)))


def known_line(here, line):
    if line == "core":
        return [here.on_core()]
    if line == "x":
        return [here.on_x(lax.rem(here.x + o, N)) for o in range(1, N)]
    return [here.on_chip(*here.chip(o * N)) for o in range(1, N)]


def head_copy(here, r, step, i):
    place = here.c * BLOCKS + here.y * N + here.z
    k = lax.rem(here.z * 2 + here.c + i // N, 2 * N)
    x = lax.rem(here.x + i, N)
    kept = (x == here.x) & (here.x * (2 * N) + k == here.me)

    def copy():
        return remote(
            r.heads.at[step, k],
            r.head_rows.at[step, place],
            r.head_send.at[step, i],
            r.head_recv.at[step, place],
            {"dp": here.x * (2 * N) + k, "tp": x},
        )

    def local():
        return pltpu.make_async_copy(
            r.heads.at[step, k], r.head_rows.at[step, place], r.head_recv.at[step, place]
        )

    return kept, copy, local


def keep(r, line, row, result):
    for c in range(KVR // 128):
        r.head_latent[line, c, row * HEADS : (row + 1) * HEADS, :] = result[:, c * 128 : (c + 1) * 128]


def value_up(here, r, line):
    def head(h):
        rows = jnp.concatenate(
            [r.head_latent.at[line, c][pl.ds(h, ROWS_DEV, stride=HEADS), :] for c in range(KVR // 128)], axis=1
        ).astype(jnp.bfloat16)
        return jnp.dot(rows, r.vup[h], preferred_element_type=jnp.float32)

    for h in range(0, HEADS, 2):
        r.heads[line, h // N, h % N // 2] = jnp.concatenate([head(h), head(h + 1)], axis=0).astype(jnp.bfloat16)

    @pl.loop(0, GROUPS)
    def _(i):
        kept, copy, local = head_copy(here, r, line, i)

        @pl.when(kept)
        def _():
            local().start()

        @pl.when(jnp.logical_not(kept))
        def _():
            copy().start()


def front_line(here, r):
    loads = {}
    for i, (name, src, dst) in enumerate(
        (
            ("lw", r.lw_hbm, r.lw),
            ("queries", r.queries_hbm, r.queries),
            ("vup", r.vup_hbm, r.vup),
            ("wo", r.wo_hbm, r.wo),
            ("wg", r.wg_hbm, r.wg.at[pl.ds(0, FF_DEV)]),
            ("wu", r.wu_hbm, r.wu),
            ("wd", r.wd_hbm, r.wd),
        )
    ):
        loads[name] = pltpu.make_async_copy(src, dst, r.load_sem.at[i])
    r.loads = loads
    slot_loads = [
        pltpu.make_async_copy(r.cache_hbm.at[j], r.cache.at[j], r.cache_sem.at[j]) for j in range(ROWS_DEV)
    ]
    for load in slot_loads:
        load.start()
    loads["lw"].start()
    barrier = pltpu.get_barrier_semaphore()
    entered = enter(here, barrier)

    moves, me = r.moves, here.me
    a0, b0, a1, b1 = moves[0, 0, me], moves[0, 1, me], moves[1, 0, me], moves[1, 1, me]
    slots, places = slot_order(moves, me)
    r.slots, r.places = slots, places
    r.wg[pl.ds(FF_DEV, SPARE), :] = jnp.zeros((SPARE, WIDTH), jnp.bfloat16)
    wide = r.tokens[...].astype(jnp.float32)
    r.tokens_wide[...] = wide
    r.latents[...] = jnp.zeros_like(r.latents)
    r.latents[:, LAT + 64 :] = jnp.broadcast_to(jnp.sum(wide * wide, axis=1, keepdims=True), (OWN, 128))

    def move(leaving, arrived, sem, part):
        rows = pl.ds(part * MOVE_ROWS, MOVE_ROWS)
        return [
            send(
                leaving.at[i, rows],
                arrived.at[i, rows],
                sem.at[0, i, part],
                sem.at[1, i, part],
                here.on_ring(o),
            )
            for i, o in enumerate((1, -1))
        ]

    for load in slot_loads:
        load.wait()
    r.leaving0[0] = r.cache[a0]
    r.leaving0[1] = r.cache[b0]
    pl.semaphore_wait(barrier, entered)
    tell(here, r.y_in, "y")
    moving0 = [move(r.leaving0, r.arrived0, r.move0_sem, part) for part in range(MOVE_PARTS)]

    loads["lw"].wait()
    r.latents[:, :LAT] = dot_rows(r.tokens[...], r.lw[...])
    copies = [
        send(
            r.latents,
            r.latent_rows.at[o - 1],
            r.latent_sem.at[0, o - 1],
            r.latent_sem.at[1, o - 1],
            here.on_x(lax.rem(here.x + o, N)),
        )
        for o in FAR_FIRST
    ]
    for name in ("queries", "vup", "wo", "wg", "wu", "wd"):
        loads[name].start()
    held = [held_first(r.lengths, moves, me, j) for j in range(ROWS_DEV)]
    held += [held_second(r.lengths, moves, me, j) for j in range(ROWS_DEV)]
    row = lax.broadcasted_iota(jnp.int32, (OWN, 128), 0)
    positions = jnp.zeros((OWN, 128), jnp.int32)
    for i in range(OWN):
        positions = jnp.where(row == i, held[i], positions)

    def held_at(step, place):
        result = held[step * ROWS_DEV]
        for j in range(1, ROWS_DEV):
            result = jnp.where(slots[place] == j, held[step * ROWS_DEV + j], result)
        return result

    held_by_place = [[held_at(step, p) for p in range(ROWS_DEV)] for step in range(STEPS)]
    yield
    hear(here, r.y_in, "y")
    tell(here, r.x_in, "x")
    for copy in copies:
        copy.wait()
    total = r.latents[...]
    for o in range(N - 1):
        total = total + r.latent_rows[o]
    scale = lax.rsqrt(total[:, LAT + 64 :] / D + epsilon)[:, :1]
    content, rotary = fresh_keys(total[:, : LAT + 64] * scale, positions)
    r.fresh[:, :KVR] = content
    r.fresh[:, KVR:] = rotary

    def fresh_row(step, place):
        return r.fresh[pl.ds(step * ROWS_DEV + slots[place], 1), :LAT].astype(jnp.bfloat16)

    loads["queries"].wait()
    r.ordered_copies = []

    def put_out(ref, place):
        copy = pltpu.make_async_copy(ref, r.ordered.at[place], r.out_sem.at[place])
        copy.start()
        r.ordered_copies.append(copy)

    for p in range(EARLY):
        first, second = held_by_place[0][p], held_by_place[1][p]
        block = with_row(r.cache[slots[p]], first, fresh_row(0, p))
        r.early_keys[p] = with_row(block, second, fresh_row(1, p))
        put_out(r.early_keys.at[p], p)
        rows = jnp.concatenate([r.queries[0, slots[p]], r.queries[1, slots[p]]], axis=0)
        step_row = lax.broadcasted_iota(jnp.int32, (2 * HEADS, 1), 0)
        live = jnp.where(step_row < HEADS, first + 1, second + 1)
        result = attend(rows, r.early_keys.at[p], live)
        keep(r, 0, p, result[:HEADS])
        keep(r, 0, EARLY + p, result[HEADS:])

    yield
    hear(here, r.x_in, "x")
    tell(here, r.core_in, "core")
    place_a, place_b = 0, 0
    for p in range(EARLY, ROWS_DEV):
        place_a = jnp.where(slots[p] == a1, p - EARLY, place_a)
        place_b = jnp.where(slots[p] == b1, p - EARLY, place_b)

    def arrive(step, keys, part, arrived, own_a, own_b, kept):
        rows = pl.ds(part * MOVE_ROWS, MOVE_ROWS)
        for p in range(EARLY, ROWS_DEV):
            block = jnp.where(
                slots[p] == own_a,
                arrived[1, rows],
                jnp.where(slots[p] == own_b, arrived[0, rows], kept(p, rows)),
            )
            keys[p - EARLY, rows] = with_row(
                block, held_by_place[step][p] - part * MOVE_ROWS, fresh_row(step, p)
            )

    moving1 = []
    for part in range(MOVE_PARTS):
        rows = pl.ds(part * MOVE_ROWS, MOVE_ROWS)
        for copy in moving0[part]:
            copy.wait()
        arrive(0, r.keys0, part, r.arrived0, a0, b0, lambda p, rows: r.cache[slots[p], rows])
        r.leaving1[0, rows] = r.keys0[place_a, rows]
        r.leaving1[1, rows] = r.keys0[place_b, rows]
        moving1.append(move(r.leaving1, r.arrived1, r.move1_sem, part))
    yield
    loads["vup"].wait()
    hear(here, r.core_in, "core")
    value_up(here, r, 0)
    yield
    for p in range(EARLY, ROWS_DEV):
        keep(
            r, 1, p - EARLY,
            attend(r.queries[0, slots[p]], r.keys0.at[p - EARLY], held_by_place[0][p] + 1),
        )

    yield
    for part in range(MOVE_PARTS):
        for copy in moving1[part]:
            copy.wait()
        arrive(1, r.keys1, part, r.arrived1, a1, b1, lambda p, rows: r.keys0[p - EARLY, rows])
    for p in range(EARLY, ROWS_DEV):
        put_out(r.keys1.at[p - EARLY], p)
        keep(
            r, 1, p,
            attend(r.queries[1, slots[p]], r.keys1.at[p - EARLY], held_by_place[1][p] + 1),
        )
    yield
    value_up(here, r, 1)
    yield


def reduce_over_groups(here, r, step, use):
    own, peer = r.own.at[step], r.peer_rows.at[use, step]
    sem = r.sum_sem.at[use, step]
    sums, rows = r.sums.at[step], r.rows.at[use, step]
    r.core_copy[use, step].wait()
    copies = {}
    for o in reversed(CHIPS):
        y, z = here.chip(o)
        k = y * N + z
        sums[k] = (own[k].astype(jnp.float32) + peer[k].astype(jnp.float32)).astype(jnp.bfloat16)
        copies[o] = send(sums.at[k], rows.at[o], sem.at[0, o], sem.at[1, o], here.on_chip(y, z))
    k = here.y * N + here.z
    total = own[k].astype(jnp.float32) + peer[k].astype(jnp.float32)
    yield
    for o in CHIPS:
        copies[o].wait()
        total = total + rows[o].astype(jnp.float32)
    return total


def project_both(here, r, step, use, lhs, weight):
    project(lhs(1 - here.c), weight, r.to_peer.at[step])
    core_sem = r.core_sem.at[use, step]
    r.core_copy[use, step] = send(
        r.to_peer.at[step], r.peer_rows.at[use, step], core_sem.at[0], core_sem.at[1], here.on_core()
    )
    project(lhs(here.c), weight, r.own.at[step])


def back_line(here, r, step):
    f32, bf16 = jnp.float32, jnp.bfloat16

    @pl.loop(0, GROUPS)
    def _(i):
        pltpu.make_async_copy(r.heads.at[step, 0], r.head_rows.at[step, i], r.head_recv.at[step, i]).wait()

    @pl.loop(0, GROUPS)
    def _(i):
        kept, copy, _ = head_copy(here, r, step, i)

        @pl.when(jnp.logical_not(kept))
        def _():
            copy().wait_send()

    rows = r.head_rows[step].astype(f32)
    for h in range(N):
        first = h % 2 * ROWS_DEV
        r.head_block[:, h * HD : (h + 1) * HD] = (
            rows[:, h // 2, first : first + ROWS_DEV].reshape(2 * HALF, HD).astype(bf16)
        )
    if step == 0:
        r.loads["wo"].wait()

    def half(ref, c):
        return ref[pl.ds(pl.multiple_of(c * HALF, HALF), HALF), :]

    project_both(here, r, step, 0, lambda c: half(r.head_block, c), r.wo[...])
    yield
    attention = yield from reduce_over_groups(here, r, step, 0)
    for i in range(ROWS_DEV):
        token = i // EARLY * ROWS_DEV + r.slots[step * EARLY + i % EARLY]
        r.line_tokens[step, i : i + 1, :] = r.tokens_wide[pl.ds(token, 1), :]
    tokens = stacked(r.line_tokens[step])[0]
    mixed = (tokens + attention).astype(bf16).astype(f32)
    r.mixed[step] = mixed

    mixed_all = r.mixed_all.at[step]
    mine = mixed_all.at[here.c, here.y, here.z]
    mine[...] = mixed.astype(bf16)
    sem, core_sem = r.gather_sem.at[step], r.gather_core.at[step]
    copies = {}
    for o in reversed(CHIPS):
        copies[o] = send(mine, mine, sem.at[0, o], sem.at[1, o], here.on_chip(*here.chip(o)))
    yield
    handed = []
    for o in (0, *NEAR_FIRST):
        for i in range(N):
            if o + i:
                copies[o * N + i].wait()
        block = mixed_all.at[here.c, lax.rem(here.y + N - o, N)]
        handed.append(send(block, block, core_sem.at[0, o], core_sem.at[1, o], here.on_core()))

    if step == 0:
        r.loads["wg"].wait()
        r.loads["wu"].wait()
    sums = (
        (r.gate_part.at[step], r.gate_rows.at[step], r.gate_sem.at[step], r.wg),
        (r.up_part.at[step], r.up_rows.at[step], r.up_sem.at[step], r.wu),
    )

    def chunk_copy(part, rows, sem, k):
        slot = lax.rem(k - here.x + N, N) - 1
        return remote(part.at[k], rows.at[slot], sem.at[0, slot], sem.at[1, slot], here.on_x(k))

    for core in (here.c, 1 - here.c):
        if core is not here.c:
            yield
            for copy in handed:
                copy.wait()
        wide = unstacked(mixed_all[core].astype(f32).reshape(BLOCKS, TILE, COLS))
        r.lhs[...] = (wide * r.gain[...].reshape(1, WIDTH)).astype(bf16)
        pieces = in_pieces(jnp.sum(wide * wide, axis=1, keepdims=True))
        for part, rows, sem, weight in sums:
            result = dot_rows(r.lhs[...], weight[...])
            if weight is r.wg:
                lane = lax.broadcasted_iota(jnp.int32, result.shape, 1)
                for i, piece in enumerate(pieces):
                    result = jnp.where(lane == FF_DEV + i, piece, result)
            part[pl.ds(2 * core, 2)] = result.astype(bf16).reshape(2, CHUNK, -1)
            for i in range(2):
                k = 2 * core + lax.rem(here.x + i, 2)

                @pl.when(k != here.x)
                def _():
                    chunk_copy(part, rows, sem, k).start()

    yield
    totals = []
    for part, rows, sem, _ in sums:
        total = part[here.x].astype(f32)
        for o in NEAR_FIRST:
            chunk_copy(part, rows, sem, lax.rem(here.x + o, N)).wait()
        for o in range(N - 1):
            total = total + rows[o].astype(f32)
        totals.append(total)
    gate, up = totals
    lane = lax.broadcasted_iota(jnp.int32, gate.shape, 1)
    squares = jnp.sum(jnp.where(lane >= FF_DEV, gate, 0.0), axis=1, keepdims=True)
    scale = lax.rsqrt(squares / D + epsilon)
    gate, up = gate[:, :FF_DEV] * scale, up * scale
    activation = r.activation.at[step]
    activation[here.x] = (gate / (1.0 + jnp.exp(-gate)) * up).astype(bf16)
    mine = activation.at[here.x]
    sem = r.act_sem.at[step]
    copies = {}
    for o in FAR_FIRST:
        x = lax.rem(here.x + o, N)
        copies[o] = send(mine, mine, sem.at[0, o - 1], sem.at[1, o - 1], here.on_x(x))
    yield
    for o in NEAR_FIRST:
        copies[o].wait()

    if step == 0:
        r.loads["wd"].wait()
    project_both(
        here, r, step, 1, lambda c: activation[pl.ds(2 * c, 2)].reshape(HALF, FF_DEV), r.wd[...]
    )
    yield
    down = yield from reduce_over_groups(here, r, step, 1)
    r.results[step * ROWS_DEV : (step + 1) * ROWS_DEV, :] = unstacked((r.mixed[step] + down)[None])
    yield


ORDER = "FFFFF00FF0110010110010111"

INPUTS = (
    "lengths", "moves", "tokens", "gain", "lw_hbm", "queries_hbm", "cache_hbm", "vup_hbm",
    "wo_hbm", "wg_hbm", "wu_hbm", "wd_hbm",
)


def layer_kernel(names, *refs):
    r = types.SimpleNamespace(**dict(zip(names, refs)))
    r.core_copy = {}
    here = Place()
    lines = {"F": front_line(here, r), "0": back_line(here, r, 0), "1": back_line(here, r, 1)}
    for name in ORDER:
        next(lines[name], None)
    for i in range(OWN):
        place = r.places[i % ROWS_DEV]
        row = place // EARLY * ROWS_DEV + i // ROWS_DEV * EARLY + lax.rem(place, EARLY)
        r.sorted_results[i : i + 1, :] = r.results[pl.ds(row, 1), :]
    r.out[...] = r.sorted_results[...].astype(jnp.bfloat16)
    for copy in r.ordered_copies:
        copy.wait()


def layer(lengths, moves, tokens, gain, lw, queries, cache, vup, wo, wg, wu, wd):
    bf16, f32 = jnp.bfloat16, jnp.float32
    vmem = pl.BlockSpec(memory_space=pltpu.VMEM)
    smem = pl.BlockSpec(memory_space=pltpu.SMEM)
    hbm = pl.BlockSpec(memory_space=pl.ANY)
    slot = cache.shape[1:]

    def dma(*shape):
        return pltpu.SemaphoreType.DMA(shape)

    def held(*shape, dtype=bf16):
        return pltpu.VMEM(shape, dtype)

    scratch = dict(
        cache=held(*cache.shape),
        lw=held(*lw.shape),
        queries=held(*queries.shape),
        vup=held(*vup.shape),
        wo=held(*wo.shape),
        wg=held(FF_DEV + SPARE, WIDTH),
        wu=held(*wu.shape),
        wd=held(*wd.shape),
        latents=held(OWN, LAT + 64 + 128, dtype=f32),
        latent_rows=held(N - 1, OWN, LAT + 64 + 128, dtype=f32),
        fresh=held(OWN, LAT + 64, dtype=f32),
        leaving0=held(2, *slot),
        leaving1=held(2, *slot),
        arrived0=held(2, *slot),
        arrived1=held(2, *slot),
        early_keys=held(EARLY, *slot),
        keys0=held(ROWS_DEV - EARLY, *slot),
        keys1=held(ROWS_DEV - EARLY, *slot),
        head_latent=held(2, KVR // 128, ROWS_DEV * HEADS, 128, dtype=f32),
        heads=held(STEPS, 2 * N, N // 2, TILE, HD),
        head_rows=held(STEPS, GROUPS, N // 2, TILE, HD),
        head_block=held(2 * HALF, N * HD),
        to_peer=held(STEPS, BLOCKS, TILE, COLS),
        own=held(STEPS, BLOCKS, TILE, COLS),
        peer_rows=held(2, STEPS, BLOCKS, TILE, COLS),
        sums=held(STEPS, BLOCKS, TILE, COLS),
        rows=held(2, STEPS, BLOCKS, TILE, COLS),
        mixed=held(STEPS, TILE, COLS, dtype=f32),
        mixed_all=held(STEPS, 2, N, N, TILE, COLS),
        lhs=held(HALF, WIDTH),
        gate_part=held(STEPS, N, CHUNK, FF_DEV + SPARE),
        up_part=held(STEPS, N, CHUNK, FF_DEV),
        gate_rows=held(STEPS, N - 1, CHUNK, FF_DEV + SPARE),
        up_rows=held(STEPS, N - 1, CHUNK, FF_DEV),
        activation=held(STEPS, N, CHUNK, FF_DEV),
        results=held(OWN, WIDTH, dtype=f32),
        sorted_results=held(OWN, WIDTH, dtype=f32),
        tokens_wide=held(OWN, WIDTH, dtype=f32),
        line_tokens=held(2, ROWS_DEV, WIDTH, dtype=f32),
        y_in=pltpu.SemaphoreType.REGULAR,
        x_in=pltpu.SemaphoreType.REGULAR,
        core_in=pltpu.SemaphoreType.REGULAR,
        load_sem=dma(7),
        cache_sem=dma(ROWS_DEV),
        latent_sem=dma(2, N - 1),
        move0_sem=dma(2, 2, MOVE_PARTS),
        move1_sem=dma(2, 2, MOVE_PARTS),
        out_sem=dma(ROWS_DEV),
        head_send=dma(STEPS, GROUPS),
        head_recv=dma(STEPS, GROUPS),
        core_sem=dma(2, STEPS, 2),
        sum_sem=dma(2, STEPS, 2, BLOCKS),
        gather_sem=dma(STEPS, 2, BLOCKS),
        gather_core=dma(STEPS, 2, N),
        gate_sem=dma(STEPS, 2, N - 1),
        up_sem=dma(STEPS, 2, N - 1),
        act_sem=dma(STEPS, 2, N - 1),
    )
    names = (*INPUTS, "out", "ordered", *scratch)

    def kernel(*refs):
        layer_kernel(names, *refs)

    return pl.pallas_call(
        kernel,
        out_shape=(
            jax.ShapeDtypeStruct((OWN, WIDTH), bf16),
            jax.ShapeDtypeStruct(cache.shape, bf16),
        ),
        in_specs=[smem, smem, vmem, vmem] + [hbm] * 8,
        out_specs=(vmem, hbm),
        scratch_shapes=list(scratch.values()),
        compiler_params=pltpu.CompilerParams(
            collective_id=0, has_side_effects=True, vmem_limit_bytes=58 * 1024 * 1024
        ),
        name="layer",
    )(lengths, moves, tokens, gain, lw, queries, cache, vup, wo, wg, wu, wd)


def finish_kernel(
    lengths, moves, group, ordered, rows, final_cache, final_rows, final_lengths, moved, slots, row_block, sems, row_sem
):
    _, places = slot_order(moves, group[0])
    loads = [pltpu.make_async_copy(ordered.at[places[j]], slots.at[j], sems.at[0, j]) for j in range(ROWS_DEV)]
    stores = [pltpu.make_async_copy(slots.at[j], final_cache.at[j], sems.at[1, j]) for j in range(ROWS_DEV)]
    loads.append(pltpu.make_async_copy(rows, row_block, row_sem.at[0]))
    stores.append(pltpu.make_async_copy(row_block, final_rows, row_sem.at[1]))
    for load in loads:
        load.start()

    def pass_on(first, last):
        for load, store in zip(loads[first:last], stores[first:last]):
            load.wait()
            store.start()

    @pl.loop(0, GROUPS)
    def _(g):
        for j in range(ROWS_DEV):
            moved[g * ROWS_DEV + j] = lengths[g * ROWS_DEV + j] + 1

    pass_on(0, 3)

    @pl.loop(0, GROUPS)
    def _(g):
        right = lax.rem(g + 1, GROUPS)
        left = lax.rem(g + GROUPS - 1, GROUPS)
        moved[g * ROWS_DEV + moves[0, 0, g]] = lengths[right * ROWS_DEV + moves[0, 1, right]] + 1
        moved[g * ROWS_DEV + moves[0, 1, g]] = lengths[left * ROWS_DEV + moves[0, 0, left]] + 1

    pass_on(3, ROWS_DEV + 1)

    @pl.loop(0, GROUPS)
    def _(g):
        for j in range(ROWS_DEV):
            final_lengths[g * ROWS_DEV + j] = moved[g * ROWS_DEV + j] + 1

    @pl.loop(0, GROUPS)
    def _(g):
        right = lax.rem(g + 1, GROUPS)
        left = lax.rem(g + GROUPS - 1, GROUPS)
        final_lengths[g * ROWS_DEV + moves[1, 0, g]] = moved[right * ROWS_DEV + moves[1, 1, right]] + 1
        final_lengths[g * ROWS_DEV + moves[1, 1, g]] = moved[left * ROWS_DEV + moves[1, 0, left]] + 1

    for store in stores:
        store.wait()


def finish(lengths, moves, group, ordered, rows):
    smem = pl.BlockSpec(memory_space=pltpu.SMEM)
    hbm = pl.BlockSpec(memory_space=pltpu.HBM)
    return pl.pallas_call(
        finish_kernel,
        out_shape=(
            jax.ShapeDtypeStruct(ordered.shape, ordered.dtype),
            jax.ShapeDtypeStruct(rows.shape, rows.dtype),
            jax.ShapeDtypeStruct(lengths.shape, jnp.int32),
        ),
        in_specs=[smem, smem, smem, hbm, hbm],
        out_specs=(hbm, hbm, smem),
        scratch_shapes=[
            pltpu.SMEM(lengths.shape, jnp.int32),
            pltpu.VMEM(ordered.shape, ordered.dtype),
            pltpu.VMEM(rows.shape, rows.dtype),
            pltpu.SemaphoreType.DMA((2, ROWS_DEV)),
            pltpu.SemaphoreType.DMA((2,)),
        ],
        compiler_params=pltpu.CompilerParams(vmem_limit_bytes=60 * 1024 * 1024),
        name="finish",
    )(lengths, moves, group, ordered, rows)


def on_device(
    latent_cache,
    lengths,
    slot_moves,
    hidden_in,
    queries,
    latent_weight,
    value_up_projection,
    out_weight,
    post_gain,
    gate_projection_matrix,
    up_weight,
    down_weight,
):
    moves = jnp.swapaxes(slot_moves, 1, 2)
    rows, ordered = layer(
        lengths,
        moves,
        hidden_in.reshape(OWN, WIDTH),
        post_gain,
        latent_weight.T,
        queries,
        latent_cache,
        value_up_projection,
        out_weight,
        gate_projection_matrix.T,
        up_weight.T,
        down_weight,
    )
    group = lax.axis_index("dp").reshape(1)
    final_cache, final_rows, final_lengths = finish(lengths, moves, group, ordered, rows)
    return (final_rows.reshape(STEPS, ROWS_DEV, WIDTH), final_cache, final_lengths)


def solution(mesh):
    return jax.shard_map(
        on_device,
        mesh=mesh,
        in_specs=(
            P("dp", None, None),
            P(),
            P(),
            P(None, "dp", "tp"),
            P(None, "dp", "tp", None),
            P("tp", None),
            P("tp", None, None),
            P("dp", "tp"),
            P("tp"),
            P("tp", "dp"),
            P("tp", "dp"),
            P("dp", "tp"),
        ),
        out_specs=(P(None, "dp", "tp"), P("dp", None, None), P()),
        check_vma=False,
    )
```

```python
import math
import types

import jax
import jax.numpy as jnp
from jax import lax
from jax.experimental import pallas as pl
from jax.experimental.pallas import tpu as pltpu
from jax.sharding import PartitionSpec as P

D = 7168
KVR = 512
ROPE = 64
HD = 128
STEPS = 2
ROWS_DEV = 8
N = 4
OWN = STEPS * ROWS_DEV
BLOCKS = N * N
HALF = BLOCKS * ROWS_DEV
WIDTH = D // N
COLS = WIDTH // 2
TILE = 2 * ROWS_DEV
FF_DEV = 576
CHUNK = 2 * HALF // N
HEADS = 32
LAT = KVR + ROPE
GROUPS = 2 * N * N
EARLY = 4
CAP = 448
MOVE_PARTS = 4
MOVE_ROWS = CAP // MOVE_PARTS
NEAR_FIRST = (1, 3, 2)
FAR_FIRST = (2, 1, 3)
HOPS = (0, 1, 2, 1)
CHIPS = sorted(range(1, N * N), key=lambda o: HOPS[o // N] + HOPS[o % N])
SPARE = 64
MESH = pl.DeviceIdType.MESH


epsilon = 1e-06


def dot_rows(lhs, rhs):
    return lax.dot_general(
        lhs, rhs, (((1,), (1,)), ((), ())), preferred_element_type=jnp.float32
    )


class Place:
    def __init__(self):
        dp = lax.axis_index("dp")
        self.x = lax.axis_index("tp")
        self.y = dp // (2 * N)
        self.z = (dp // 2) % N
        self.c = dp % 2
        self.me = dp

    def on_chip(self, y, z):
        return {"dp": y * (2 * N) + z * 2 + self.c, "tp": self.x}

    def on_core(self):
        return {"dp": self.me + 1 - 2 * self.c, "tp": self.x}

    def on_x(self, k):
        return {"dp": self.me, "tp": k}

    def on_ring(self, o):
        return {"dp": lax.rem(self.me + o + GROUPS, GROUPS), "tp": self.x}

    def chip(self, offset):
        return lax.rem(self.y + offset // N, N), lax.rem(self.z + offset % N, N)


def remote(src, dst, send_sem, recv_sem, device):
    return pltpu.make_async_remote_copy(
        src_ref=src,
        dst_ref=dst,
        send_sem=send_sem,
        recv_sem=recv_sem,
        device_id=device,
        device_id_type=MESH,
    )


def send(*args):
    copy = remote(*args)
    copy.start()
    return copy


def stacked(rows):
    left = rows[:, :COLS].reshape(-1, ROWS_DEV, COLS)
    right = rows[:, COLS:].reshape(-1, ROWS_DEV, COLS)
    return jnp.concatenate([left, right], axis=1)


def unstacked(blocks):
    left = blocks[:, :ROWS_DEV].reshape(-1, COLS)
    right = blocks[:, ROWS_DEV:].reshape(-1, COLS)
    return jnp.concatenate([left, right], axis=1)


def project(lhs, weight, out):
    for start in range(0, COLS, 256):
        width = min(256, COLS - start)
        parts = [
            jnp.dot(
                lhs, weight[:, first + start : first + start + width], preferred_element_type=jnp.float32
            ).reshape(-1, ROWS_DEV, width)
            for first in (0, COLS)
        ]
        out[:, :, start : start + width] = jnp.concatenate(parts, axis=1).astype(jnp.bfloat16)


def in_pieces(value):
    pieces = []
    for _ in range(3):
        piece = value.astype(jnp.bfloat16).astype(jnp.float32)
        pieces.append(piece)
        value = value - piece
    return pieces


def source_of(moves, step, group, slot):
    right = lax.rem(group + 1, GROUPS)
    left = lax.rem(group + GROUPS - 1, GROUPS)
    to_right = slot == moves[step, 0, group]
    to_left = slot == moves[step, 1, group]
    source_group = jnp.where(to_right, right, jnp.where(to_left, left, group))
    source_slot = jnp.where(
        to_right, moves[step, 1, right], jnp.where(to_left, moves[step, 0, left], slot)
    )
    return source_group, source_slot


def held_first(lengths, moves, group, slot):
    source_group, source_slot = source_of(moves, 0, group, slot)
    return lengths[source_group * ROWS_DEV + source_slot]


def held_second(lengths, moves, group, slot):
    source_group, source_slot = source_of(moves, 1, group, slot)
    return held_first(lengths, moves, source_group, source_slot) + 1


def slot_order(moves, group):
    free_before, slots, places = 0, [0] * ROWS_DEV, []
    for j in range(ROWS_DEV):
        moved = (
            (j == moves[0, 0, group])
            | (j == moves[0, 1, group])
            | (j == moves[1, 0, group])
            | (j == moves[1, 1, group])
        )
        early = jnp.where(moved | (free_before >= EARLY), 0, 1)
        place = jnp.where(early == 1, free_before, EARLY + j - free_before)
        places.append(place)
        slots = [jnp.where(place == p, j, slots[p]) for p in range(ROWS_DEV)]
        free_before = free_before + early
    return slots, places


def with_row(block, position, row):
    rows = lax.broadcasted_iota(jnp.int32, block.shape, 0)
    return jnp.where(rows == position, jnp.broadcast_to(row, block.shape), block)


def attend(query_rows, keys, live):
    scores = dot_rows(query_rows, keys[...]) * (HD + ROPE) ** (-0.5)
    positions = lax.broadcasted_iota(jnp.int32, scores.shape, 1)
    scores = jnp.where(positions < live, scores, -1e30)
    powers = jnp.exp(scores - jnp.max(scores, axis=1, keepdims=True))
    weights = (powers / jnp.sum(powers, axis=1, keepdims=True)).astype(jnp.bfloat16)
    return jnp.dot(weights, keys[:, :KVR], preferred_element_type=jnp.float32)


def fresh_keys(latent, positions):
    content = latent[:, :KVR]
    content = content * lax.rsqrt(jnp.mean(content * content, axis=1, keepdims=True) + epsilon)
    rotary = latent[:, KVR:]
    lane = lax.broadcasted_iota(jnp.int32, rotary.shape, 1)
    half = ROPE // 2
    power = lax.rem(lane, half).astype(jnp.float32) * (-2.0 / ROPE * math.log(10000.0))
    angles = positions.astype(jnp.float32) * jnp.exp(power)
    turned = jnp.where(lane < half, -pltpu.roll(rotary, 128 - half, 1), pltpu.roll(rotary, half, 1))
    return content, rotary * jnp.cos(angles) + turned * jnp.sin(angles)


def enter(here, barrier):
    devices = [here.on_ring(1), here.on_ring(-1), here.on_core()]
    for o in range(1, N):
        devices += [here.on_x(lax.rem(here.x + o, N)), here.on_chip(*here.chip(o)), here.on_chip(*here.chip(o * N))]
    for device in devices:
        pl.semaphore_signal(barrier, inc=1, device_id=device, device_id_type=MESH)
    return len(devices)


def tell(here, sem, line):
    for device in known_line(here, line):
        pl.semaphore_signal(sem, inc=1, device_id=device, device_id_type=MESH)


def hear(here, sem, line):
    pl.semaphore_wait(sem, len(known_line(here, line)))


def known_line(here, line):
    if line == "core":
        return [here.on_core()]
    if line == "x":
        return [here.on_x(lax.rem(here.x + o, N)) for o in range(1, N)]
    return [here.on_chip(*here.chip(o * N)) for o in range(1, N)]


def head_copy(here, r, step, i):
    place = here.c * BLOCKS + here.y * N + here.z
    k = lax.rem(here.z * 2 + here.c + i // N, 2 * N)
    x = lax.rem(here.x + i, N)
    kept = (x == here.x) & (here.x * (2 * N) + k == here.me)

    def copy():
        return remote(
            r.heads.at[step, k],
            r.head_rows.at[step, place],
            r.head_send.at[step, i],
            r.head_recv.at[step, place],
            {"dp": here.x * (2 * N) + k, "tp": x},
        )

    def local():
        return pltpu.make_async_copy(
            r.heads.at[step, k], r.head_rows.at[step, place], r.head_recv.at[step, place]
        )

    return kept, copy, local


def keep(r, line, row, result):
    for c in range(KVR // 128):
        r.head_latent[line, c, row * HEADS : (row + 1) * HEADS, :] = result[:, c * 128 : (c + 1) * 128]


def value_up(here, r, line):
    def head(h):
        rows = jnp.concatenate(
            [r.head_latent.at[line, c][pl.ds(h, ROWS_DEV, stride=HEADS), :] for c in range(KVR // 128)], axis=1
        ).astype(jnp.bfloat16)
        return jnp.dot(rows, r.vup[h], preferred_element_type=jnp.float32)

    for h in range(0, HEADS, 2):
        r.heads[line, h // N, h % N // 2] = jnp.concatenate([head(h), head(h + 1)], axis=0).astype(jnp.bfloat16)

    @pl.loop(0, GROUPS)
    def _(i):
        kept, copy, local = head_copy(here, r, line, i)

        @pl.when(kept)
        def _():
            local().start()

        @pl.when(jnp.logical_not(kept))
        def _():
            copy().start()


def front_line(here, r):
    loads = {}
    for i, (name, src, dst) in enumerate(
        (
            ("lw", r.lw_hbm, r.lw),
            ("queries", r.queries_hbm, r.queries),
            ("vup", r.vup_hbm, r.vup),
            ("wo", r.wo_hbm, r.wo),
            ("wg", r.wg_hbm, r.wg.at[pl.ds(0, FF_DEV)]),
            ("wu", r.wu_hbm, r.wu),
            ("wd", r.wd_hbm, r.wd),
        )
    ):
        loads[name] = pltpu.make_async_copy(src, dst, r.load_sem.at[i])
    r.loads = loads
    slot_loads = [
        pltpu.make_async_copy(r.cache_hbm.at[j], r.cache.at[j], r.cache_sem.at[j]) for j in range(ROWS_DEV)
    ]
    for load in slot_loads:
        load.start()
    loads["lw"].start()
    barrier = pltpu.get_barrier_semaphore()
    entered = enter(here, barrier)

    moves, me = r.moves, here.me
    a0, b0, a1, b1 = moves[0, 0, me], moves[0, 1, me], moves[1, 0, me], moves[1, 1, me]
    slots, places = slot_order(moves, me)
    r.slots, r.places = slots, places
    r.wg[pl.ds(FF_DEV, SPARE), :] = jnp.zeros((SPARE, WIDTH), jnp.bfloat16)
    wide = r.tokens[...].astype(jnp.float32)
    r.tokens_wide[...] = wide
    r.latents[...] = jnp.zeros_like(r.latents)
    r.latents[:, LAT + 64 :] = jnp.broadcast_to(jnp.sum(wide * wide, axis=1, keepdims=True), (OWN, 128))

    def move(leaving, arrived, sem, part):
        rows = pl.ds(part * MOVE_ROWS, MOVE_ROWS)
        return [
            send(
                leaving.at[i, rows],
                arrived.at[i, rows],
                sem.at[0, i, part],
                sem.at[1, i, part],
                here.on_ring(o),
            )
            for i, o in enumerate((1, -1))
        ]

    for load in slot_loads:
        load.wait()
    r.leaving0[0] = r.cache[a0]
    r.leaving0[1] = r.cache[b0]
    pl.semaphore_wait(barrier, entered)
    tell(here, r.y_in, "y")
    moving0 = [move(r.leaving0, r.arrived0, r.move0_sem, part) for part in range(MOVE_PARTS)]

    loads["lw"].wait()
    r.latents[:, :LAT] = dot_rows(r.tokens[...], r.lw[...])
    copies = [
        send(
            r.latents,
            r.latent_rows.at[o - 1],
            r.latent_sem.at[0, o - 1],
            r.latent_sem.at[1, o - 1],
            here.on_x(lax.rem(here.x + o, N)),
        )
        for o in FAR_FIRST
    ]
    for name in ("queries", "vup", "wo", "wg", "wu", "wd"):
        loads[name].start()
    held = [held_first(r.lengths, moves, me, j) for j in range(ROWS_DEV)]
    held += [held_second(r.lengths, moves, me, j) for j in range(ROWS_DEV)]
    row = lax.broadcasted_iota(jnp.int32, (OWN, 128), 0)
    positions = jnp.zeros((OWN, 128), jnp.int32)
    for i in range(OWN):
        positions = jnp.where(row == i, held[i], positions)

    def held_at(step, place):
        result = held[step * ROWS_DEV]
        for j in range(1, ROWS_DEV):
            result = jnp.where(slots[place] == j, held[step * ROWS_DEV + j], result)
        return result

    held_by_place = [[held_at(step, p) for p in range(ROWS_DEV)] for step in range(STEPS)]
    yield
    hear(here, r.y_in, "y")
    tell(here, r.x_in, "x")
    for copy in copies:
        copy.wait()
    total = r.latents[...]
    for o in range(N - 1):
        total = total + r.latent_rows[o]
    scale = lax.rsqrt(total[:, LAT + 64 :] / D + epsilon)[:, :1]
    content, rotary = fresh_keys(total[:, : LAT + 64] * scale, positions)
    r.fresh[:, :KVR] = content
    r.fresh[:, KVR:] = rotary

    def fresh_row(step, place):
        return r.fresh[pl.ds(step * ROWS_DEV + slots[place], 1), :LAT].astype(jnp.bfloat16)

    loads["queries"].wait()
    for p in range(EARLY):
        first, second = held_by_place[0][p], held_by_place[1][p]
        block = with_row(r.cache[slots[p]], first, fresh_row(0, p))
        r.ordered[p][...] = with_row(block, second, fresh_row(1, p))
        rows = jnp.concatenate([r.queries[0, slots[p]], r.queries[1, slots[p]]], axis=0)
        step_row = lax.broadcasted_iota(jnp.int32, (2 * HEADS, 1), 0)
        live = jnp.where(step_row < HEADS, first + 1, second + 1)
        result = attend(rows, r.ordered[p], live)
        keep(r, 0, p, result[:HEADS])
        keep(r, 0, EARLY + p, result[HEADS:])

    yield
    hear(here, r.x_in, "x")
    tell(here, r.core_in, "core")
    place_a, place_b = 0, 0
    for p in range(EARLY, ROWS_DEV):
        place_a = jnp.where(slots[p] == a1, p - EARLY, place_a)
        place_b = jnp.where(slots[p] == b1, p - EARLY, place_b)

    def arrive(step, keys, part, arrived, own_a, own_b, kept):
        rows = pl.ds(part * MOVE_ROWS, MOVE_ROWS)
        for p in range(EARLY, ROWS_DEV):
            block = jnp.where(
                slots[p] == own_a,
                arrived[1, rows],
                jnp.where(slots[p] == own_b, arrived[0, rows], kept(p, rows)),
            )
            keys[p][rows] = with_row(
                block, held_by_place[step][p] - part * MOVE_ROWS, fresh_row(step, p)
            )

    moving1 = []
    for part in range(MOVE_PARTS):
        rows = pl.ds(part * MOVE_ROWS, MOVE_ROWS)
        for copy in moving0[part]:
            copy.wait()
        arrive(0, {p: r.keys0.at[p - EARLY] for p in range(EARLY, ROWS_DEV)}, part, r.arrived0, a0, b0, lambda p, rows: r.cache[slots[p], rows])
        r.leaving1[0, rows] = r.keys0[place_a, rows]
        r.leaving1[1, rows] = r.keys0[place_b, rows]
        moving1.append(move(r.leaving1, r.arrived1, r.move1_sem, part))
    yield
    loads["vup"].wait()
    hear(here, r.core_in, "core")
    value_up(here, r, 0)
    yield
    for p in range(EARLY, ROWS_DEV):
        keep(
            r, 1, p - EARLY,
            attend(r.queries[0, slots[p]], r.keys0.at[p - EARLY], held_by_place[0][p] + 1),
        )

    yield
    for part in range(MOVE_PARTS):
        for copy in moving1[part]:
            copy.wait()
        arrive(1, r.ordered, part, r.arrived1, a1, b1, lambda p, rows: r.keys0[p - EARLY, rows])
    for p in range(EARLY, ROWS_DEV):
        keep(
            r, 1, p,
            attend(r.queries[1, slots[p]], r.ordered[p], held_by_place[1][p] + 1),
        )
    yield
    value_up(here, r, 1)
    yield


def reduce_over_groups(here, r, step, use):
    own, peer = r.own.at[step], r.peer_rows.at[use, step]
    sem = r.sum_sem.at[use, step]
    sums, rows = r.sums.at[step], r.rows.at[use, step]
    r.core_copy[use, step].wait()
    copies = {}
    for o in reversed(CHIPS):
        y, z = here.chip(o)
        k = y * N + z
        sums[k] = (own[k].astype(jnp.float32) + peer[k].astype(jnp.float32)).astype(jnp.bfloat16)
        copies[o] = send(sums.at[k], rows.at[o], sem.at[0, o], sem.at[1, o], here.on_chip(y, z))
    k = here.y * N + here.z
    total = own[k].astype(jnp.float32) + peer[k].astype(jnp.float32)
    yield
    for o in CHIPS:
        copies[o].wait()
        total = total + rows[o].astype(jnp.float32)
    return total


def project_both(here, r, step, use, lhs, weight):
    project(lhs(1 - here.c), weight, r.to_peer.at[step])
    core_sem = r.core_sem.at[use, step]
    r.core_copy[use, step] = send(
        r.to_peer.at[step], r.peer_rows.at[use, step], core_sem.at[0], core_sem.at[1], here.on_core()
    )
    project(lhs(here.c), weight, r.own.at[step])


def back_line(here, r, step):
    f32, bf16 = jnp.float32, jnp.bfloat16

    @pl.loop(0, GROUPS)
    def _(i):
        pltpu.make_async_copy(r.heads.at[step, 0], r.head_rows.at[step, i], r.head_recv.at[step, i]).wait()

    @pl.loop(0, GROUPS)
    def _(i):
        kept, copy, _ = head_copy(here, r, step, i)

        @pl.when(jnp.logical_not(kept))
        def _():
            copy().wait_send()

    rows = r.head_rows[step].astype(f32)
    for h in range(N):
        first = h % 2 * ROWS_DEV
        r.head_block[:, h * HD : (h + 1) * HD] = (
            rows[:, h // 2, first : first + ROWS_DEV].reshape(2 * HALF, HD).astype(bf16)
        )
    if step == 0:
        r.loads["wo"].wait()

    def half(ref, c):
        return ref[pl.ds(pl.multiple_of(c * HALF, HALF), HALF), :]

    project_both(here, r, step, 0, lambda c: half(r.head_block, c), r.wo[...])
    yield
    attention = yield from reduce_over_groups(here, r, step, 0)
    for i in range(ROWS_DEV):
        token = i // EARLY * ROWS_DEV + r.slots[step * EARLY + i % EARLY]
        r.line_tokens[step, i : i + 1, :] = r.tokens_wide[pl.ds(token, 1), :]
    tokens = stacked(r.line_tokens[step])[0]
    mixed = (tokens + attention).astype(bf16).astype(f32)
    r.mixed[step] = mixed

    mixed_all = r.mixed_all.at[step]
    mine = mixed_all.at[here.c, here.y, here.z]
    mine[...] = mixed.astype(bf16)
    sem, core_sem = r.gather_sem.at[step], r.gather_core.at[step]
    copies = {}
    for o in reversed(CHIPS):
        copies[o] = send(mine, mine, sem.at[0, o], sem.at[1, o], here.on_chip(*here.chip(o)))
    yield
    handed = []
    for o in (0, *NEAR_FIRST):
        for i in range(N):
            if o + i:
                copies[o * N + i].wait()
        block = mixed_all.at[here.c, lax.rem(here.y + N - o, N)]
        handed.append(send(block, block, core_sem.at[0, o], core_sem.at[1, o], here.on_core()))

    if step == 0:
        r.loads["wg"].wait()
        r.loads["wu"].wait()
    sums = (
        (r.gate_part.at[step], r.gate_rows.at[step], r.gate_sem.at[step], r.wg),
        (r.up_part.at[step], r.up_rows.at[step], r.up_sem.at[step], r.wu),
    )

    def chunk_copy(part, rows, sem, k):
        slot = lax.rem(k - here.x + N, N) - 1
        return remote(part.at[k], rows.at[slot], sem.at[0, slot], sem.at[1, slot], here.on_x(k))

    for core in (here.c, 1 - here.c):
        if core is not here.c:
            yield
            for copy in handed:
                copy.wait()
        wide = unstacked(mixed_all[core].astype(f32).reshape(BLOCKS, TILE, COLS))
        r.lhs[...] = (wide * r.gain[...].reshape(1, WIDTH)).astype(bf16)
        pieces = in_pieces(jnp.sum(wide * wide, axis=1, keepdims=True))
        for part, rows, sem, weight in sums:
            result = dot_rows(r.lhs[...], weight[...])
            if weight is r.wg:
                lane = lax.broadcasted_iota(jnp.int32, result.shape, 1)
                for i, piece in enumerate(pieces):
                    result = jnp.where(lane == FF_DEV + i, piece, result)
            part[pl.ds(2 * core, 2)] = result.astype(bf16).reshape(2, CHUNK, -1)
            for i in range(2):
                k = 2 * core + lax.rem(here.x + i, 2)

                @pl.when(k != here.x)
                def _():
                    chunk_copy(part, rows, sem, k).start()

    yield
    totals = []
    for part, rows, sem, _ in sums:
        total = part[here.x].astype(f32)
        for o in NEAR_FIRST:
            chunk_copy(part, rows, sem, lax.rem(here.x + o, N)).wait()
        for o in range(N - 1):
            total = total + rows[o].astype(f32)
        totals.append(total)
    gate, up = totals
    lane = lax.broadcasted_iota(jnp.int32, gate.shape, 1)
    squares = jnp.sum(jnp.where(lane >= FF_DEV, gate, 0.0), axis=1, keepdims=True)
    scale = lax.rsqrt(squares / D + epsilon)
    gate, up = gate[:, :FF_DEV] * scale, up * scale
    activation = r.activation.at[step]
    activation[here.x] = (gate / (1.0 + jnp.exp(-gate)) * up).astype(bf16)
    mine = activation.at[here.x]
    sem = r.act_sem.at[step]
    copies = {}
    for o in FAR_FIRST:
        x = lax.rem(here.x + o, N)
        copies[o] = send(mine, mine, sem.at[0, o - 1], sem.at[1, o - 1], here.on_x(x))
    yield
    for o in NEAR_FIRST:
        copies[o].wait()

    if step == 0:
        r.loads["wd"].wait()
    project_both(
        here, r, step, 1, lambda c: activation[pl.ds(2 * c, 2)].reshape(HALF, FF_DEV), r.wd[...]
    )
    yield
    down = yield from reduce_over_groups(here, r, step, 1)
    r.results[step * ROWS_DEV : (step + 1) * ROWS_DEV, :] = unstacked((r.mixed[step] + down)[None])
    yield


ORDER = "FFFFF00FF0110010110010111"

INPUTS = (
    "lengths", "moves", "tokens", "gain", "lw_hbm", "queries_hbm", "cache_hbm", "vup_hbm",
    "wo_hbm", "wg_hbm", "wu_hbm", "wd_hbm",
)


def layer_kernel(names, *refs):
    r = types.SimpleNamespace(**dict(zip(names, refs)))
    r.core_copy = {}
    r.ordered = [getattr(r, f"ordered{p}") for p in range(ROWS_DEV)]
    here = Place()
    lines = {"F": front_line(here, r), "0": back_line(here, r, 0), "1": back_line(here, r, 1)}
    for name in ORDER:
        next(lines[name], None)
    for i in range(OWN):
        place = r.places[i % ROWS_DEV]
        row = place // EARLY * ROWS_DEV + i // ROWS_DEV * EARLY + lax.rem(place, EARLY)
        r.sorted_results[i : i + 1, :] = r.results[pl.ds(row, 1), :]
    r.out[...] = r.sorted_results[...].astype(jnp.bfloat16)


def layer(lengths, moves, tokens, gain, lw, queries, cache, vup, wo, wg, wu, wd):
    bf16, f32 = jnp.bfloat16, jnp.float32
    vmem = pl.BlockSpec(memory_space=pltpu.VMEM)
    smem = pl.BlockSpec(memory_space=pltpu.SMEM)
    hbm = pl.BlockSpec(memory_space=pl.ANY)
    slot = cache.shape[1:]

    def dma(*shape):
        return pltpu.SemaphoreType.DMA(shape)

    def held(*shape, dtype=bf16):
        return pltpu.VMEM(shape, dtype)

    scratch = dict(
        cache=held(*cache.shape),
        lw=held(*lw.shape),
        queries=held(*queries.shape),
        vup=held(*vup.shape),
        wo=held(*wo.shape),
        wg=held(FF_DEV + SPARE, WIDTH),
        wu=held(*wu.shape),
        wd=held(*wd.shape),
        latents=held(OWN, LAT + 64 + 128, dtype=f32),
        latent_rows=held(N - 1, OWN, LAT + 64 + 128, dtype=f32),
        fresh=held(OWN, LAT + 64, dtype=f32),
        leaving0=held(2, *slot),
        leaving1=held(2, *slot),
        arrived0=held(2, *slot),
        arrived1=held(2, *slot),
        keys0=held(ROWS_DEV - EARLY, *slot),
        head_latent=held(2, KVR // 128, ROWS_DEV * HEADS, 128, dtype=f32),
        heads=held(STEPS, 2 * N, N // 2, TILE, HD),
        head_rows=held(STEPS, GROUPS, N // 2, TILE, HD),
        head_block=held(2 * HALF, N * HD),
        to_peer=held(STEPS, BLOCKS, TILE, COLS),
        own=held(STEPS, BLOCKS, TILE, COLS),
        peer_rows=held(2, STEPS, BLOCKS, TILE, COLS),
        sums=held(STEPS, BLOCKS, TILE, COLS),
        rows=held(2, STEPS, BLOCKS, TILE, COLS),
        mixed=held(STEPS, TILE, COLS, dtype=f32),
        mixed_all=held(STEPS, 2, N, N, TILE, COLS),
        lhs=held(HALF, WIDTH),
        gate_part=held(STEPS, N, CHUNK, FF_DEV + SPARE),
        up_part=held(STEPS, N, CHUNK, FF_DEV),
        gate_rows=held(STEPS, N - 1, CHUNK, FF_DEV + SPARE),
        up_rows=held(STEPS, N - 1, CHUNK, FF_DEV),
        activation=held(STEPS, N, CHUNK, FF_DEV),
        results=held(OWN, WIDTH, dtype=f32),
        sorted_results=held(OWN, WIDTH, dtype=f32),
        tokens_wide=held(OWN, WIDTH, dtype=f32),
        line_tokens=held(2, ROWS_DEV, WIDTH, dtype=f32),
        y_in=pltpu.SemaphoreType.REGULAR,
        x_in=pltpu.SemaphoreType.REGULAR,
        core_in=pltpu.SemaphoreType.REGULAR,
        load_sem=dma(7),
        cache_sem=dma(ROWS_DEV),
        latent_sem=dma(2, N - 1),
        move0_sem=dma(2, 2, MOVE_PARTS),
        move1_sem=dma(2, 2, MOVE_PARTS),
        head_send=dma(STEPS, GROUPS),
        head_recv=dma(STEPS, GROUPS),
        core_sem=dma(2, STEPS, 2),
        sum_sem=dma(2, STEPS, 2, BLOCKS),
        gather_sem=dma(STEPS, 2, BLOCKS),
        gather_core=dma(STEPS, 2, N),
        gate_sem=dma(STEPS, 2, N - 1),
        up_sem=dma(STEPS, 2, N - 1),
        act_sem=dma(STEPS, 2, N - 1),
    )
    names = (*INPUTS, "out", *(f"ordered{p}" for p in range(ROWS_DEV)), *scratch)

    def kernel(*refs):
        layer_kernel(names, *refs)

    return pl.pallas_call(
        kernel,
        out_shape=(
            jax.ShapeDtypeStruct((OWN, WIDTH), bf16),
            *[jax.ShapeDtypeStruct(slot, bf16)] * ROWS_DEV,
        ),
        in_specs=[smem, smem, vmem, vmem] + [hbm] * 8,
        out_specs=(vmem, *[vmem] * ROWS_DEV),
        scratch_shapes=list(scratch.values()),
        compiler_params=pltpu.CompilerParams(
            collective_id=0, has_side_effects=True, vmem_limit_bytes=49 * 1024 * 1024
        ),
        name="layer",
    )(lengths, moves, tokens, gain, lw, queries, cache, vup, wo, wg, wu, wd)


def finish_kernel(lengths, moves, group, rows, *refs):
    ordered, (final_cache, final_rows, final_lengths, moved, sems) = refs[:ROWS_DEV], refs[ROWS_DEV:]
    slots, _ = slot_order(moves, group[0])
    stores = [
        pltpu.make_async_copy(ordered[p], final_cache.at[slots[p]], sems.at[p]) for p in range(ROWS_DEV)
    ]
    stores.append(pltpu.make_async_copy(rows, final_rows, sems.at[ROWS_DEV]))
    for store in stores:
        store.start()

    @pl.loop(0, GROUPS)
    def _(g):
        for j in range(ROWS_DEV):
            moved[g * ROWS_DEV + j] = lengths[g * ROWS_DEV + j] + 1


    @pl.loop(0, GROUPS)
    def _(g):
        right = lax.rem(g + 1, GROUPS)
        left = lax.rem(g + GROUPS - 1, GROUPS)
        moved[g * ROWS_DEV + moves[0, 0, g]] = lengths[right * ROWS_DEV + moves[0, 1, right]] + 1
        moved[g * ROWS_DEV + moves[0, 1, g]] = lengths[left * ROWS_DEV + moves[0, 0, left]] + 1

    @pl.loop(0, GROUPS)
    def _(g):
        for j in range(ROWS_DEV):
            final_lengths[g * ROWS_DEV + j] = moved[g * ROWS_DEV + j] + 1

    @pl.loop(0, GROUPS)
    def _(g):
        right = lax.rem(g + 1, GROUPS)
        left = lax.rem(g + GROUPS - 1, GROUPS)
        final_lengths[g * ROWS_DEV + moves[1, 0, g]] = moved[right * ROWS_DEV + moves[1, 1, right]] + 1
        final_lengths[g * ROWS_DEV + moves[1, 1, g]] = moved[left * ROWS_DEV + moves[1, 0, left]] + 1

    for store in stores:
        store.wait()


def finish(lengths, moves, group, ordered, rows):
    smem = pl.BlockSpec(memory_space=pltpu.SMEM)
    hbm = pl.BlockSpec(memory_space=pltpu.HBM)
    vmem = pl.BlockSpec(memory_space=pltpu.VMEM)
    return pl.pallas_call(
        finish_kernel,
        out_shape=(
            jax.ShapeDtypeStruct((ROWS_DEV, *ordered[0].shape), ordered[0].dtype),
            jax.ShapeDtypeStruct(rows.shape, rows.dtype),
            jax.ShapeDtypeStruct(lengths.shape, jnp.int32),
        ),
        in_specs=[smem, smem, smem, vmem] + [vmem] * ROWS_DEV,
        out_specs=(hbm, hbm, smem),
        scratch_shapes=[
            pltpu.SMEM(lengths.shape, jnp.int32),
            pltpu.SemaphoreType.DMA((ROWS_DEV + 1,)),
        ],
        compiler_params=pltpu.CompilerParams(vmem_limit_bytes=8 * 1024 * 1024),
        name="finish",
    )(lengths, moves, group, rows, *ordered)


def on_device(
    latent_cache,
    lengths,
    slot_moves,
    hidden_in,
    queries,
    latent_weight,
    value_up_projection,
    out_weight,
    post_gain,
    gate_projection_matrix,
    up_weight,
    down_weight,
):
    moves = jnp.swapaxes(slot_moves, 1, 2)
    rows, *ordered = layer(
        lengths,
        moves,
        hidden_in.reshape(OWN, WIDTH),
        post_gain,
        latent_weight.T,
        queries,
        latent_cache,
        value_up_projection,
        out_weight,
        gate_projection_matrix.T,
        up_weight.T,
        down_weight,
    )
    group = lax.axis_index("dp").reshape(1)
    final_cache, final_rows, final_lengths = finish(lengths, moves, group, ordered, rows)
    return (final_rows.reshape(STEPS, ROWS_DEV, WIDTH), final_cache, final_lengths)


def solution(mesh):
    return jax.shard_map(
        on_device,
        mesh=mesh,
        in_specs=(
            P("dp", None, None),
            P(),
            P(),
            P(None, "dp", "tp"),
            P(None, "dp", "tp", None),
            P("tp", None),
            P("tp", None, None),
            P("dp", "tp"),
            P("tp"),
            P("tp", "dp"),
            P("tp", "dp"),
            P("dp", "tp"),
        ),
        out_specs=(P(None, "dp", "tp"), P("dp", None, None), P()),
        check_vma=False,
    )
```

```python
import math
import types

import jax
import jax.numpy as jnp
from jax import lax
from jax.experimental import pallas as pl
from jax.experimental.pallas import tpu as pltpu
from jax.sharding import PartitionSpec as P

D = 7168
KVR = 512
ROPE = 64
HD = 128
STEPS = 2
ROWS_DEV = 8
N = 4
OWN = STEPS * ROWS_DEV
BLOCKS = N * N
HALF = BLOCKS * ROWS_DEV
WIDTH = D // N
COLS = WIDTH // 2
TILE = 2 * ROWS_DEV
FF_DEV = 576
CHUNK = 2 * HALF // N
HEADS = 32
LAT = KVR + ROPE
GROUPS = 2 * N * N
EARLY = 4
CAP = 448
MOVE_PARTS = 4
MOVE_ROWS = CAP // MOVE_PARTS
NEAR_FIRST = (1, 3, 2)
FAR_FIRST = (2, 1, 3)
HOPS = (0, 1, 2, 1)
CHIPS = sorted(range(1, N * N), key=lambda o: HOPS[o // N] + HOPS[o % N])
SPARE = 64
MESH = pl.DeviceIdType.MESH


epsilon = 1e-06


def dot_rows(lhs, rhs):
    return lax.dot_general(
        lhs, rhs, (((1,), (1,)), ((), ())), preferred_element_type=jnp.float32
    )


class Place:
    def __init__(self):
        dp = lax.axis_index("dp")
        self.x = lax.axis_index("tp")
        self.y = dp // (2 * N)
        self.z = (dp // 2) % N
        self.c = dp % 2
        self.me = dp

    def on_chip(self, y, z):
        return {"dp": y * (2 * N) + z * 2 + self.c, "tp": self.x}

    def on_core(self):
        return {"dp": self.me + 1 - 2 * self.c, "tp": self.x}

    def on_x(self, k):
        return {"dp": self.me, "tp": k}

    def on_ring(self, o):
        return {"dp": lax.rem(self.me + o + GROUPS, GROUPS), "tp": self.x}

    def chip(self, offset):
        return lax.rem(self.y + offset // N, N), lax.rem(self.z + offset % N, N)


def remote(src, dst, send_sem, recv_sem, device):
    return pltpu.make_async_remote_copy(
        src_ref=src,
        dst_ref=dst,
        send_sem=send_sem,
        recv_sem=recv_sem,
        device_id=device,
        device_id_type=MESH,
    )


def send(*args):
    copy = remote(*args)
    copy.start()
    return copy


def stacked(rows):
    left = rows[:, :COLS].reshape(-1, ROWS_DEV, COLS)
    right = rows[:, COLS:].reshape(-1, ROWS_DEV, COLS)
    return jnp.concatenate([left, right], axis=1)


def unstacked(blocks):
    left = blocks[:, :ROWS_DEV].reshape(-1, COLS)
    right = blocks[:, ROWS_DEV:].reshape(-1, COLS)
    return jnp.concatenate([left, right], axis=1)


def project(lhs, weight, out):
    for start in range(0, COLS, 256):
        width = min(256, COLS - start)
        parts = [
            jnp.dot(
                lhs, weight[:, first + start : first + start + width], preferred_element_type=jnp.float32
            ).reshape(-1, ROWS_DEV, width)
            for first in (0, COLS)
        ]
        out[:, :, start : start + width] = jnp.concatenate(parts, axis=1).astype(jnp.bfloat16)


def in_pieces(value):
    pieces = []
    for _ in range(3):
        piece = value.astype(jnp.bfloat16).astype(jnp.float32)
        pieces.append(piece)
        value = value - piece
    return pieces


def source_of(moves, step, group, slot):
    right = lax.rem(group + 1, GROUPS)
    left = lax.rem(group + GROUPS - 1, GROUPS)
    to_right = slot == moves[step, 0, group]
    to_left = slot == moves[step, 1, group]
    source_group = jnp.where(to_right, right, jnp.where(to_left, left, group))
    source_slot = jnp.where(
        to_right, moves[step, 1, right], jnp.where(to_left, moves[step, 0, left], slot)
    )
    return source_group, source_slot


def held_first(lengths, moves, group, slot):
    source_group, source_slot = source_of(moves, 0, group, slot)
    return lengths[source_group * ROWS_DEV + source_slot]


def held_second(lengths, moves, group, slot):
    source_group, source_slot = source_of(moves, 1, group, slot)
    return held_first(lengths, moves, source_group, source_slot) + 1


def slot_order(moves, group):
    free_before, slots, places = 0, [0] * ROWS_DEV, []
    for j in range(ROWS_DEV):
        moved = (
            (j == moves[0, 0, group])
            | (j == moves[0, 1, group])
            | (j == moves[1, 0, group])
            | (j == moves[1, 1, group])
        )
        early = jnp.where(moved | (free_before >= EARLY), 0, 1)
        place = jnp.where(early == 1, free_before, EARLY + j - free_before)
        places.append(place)
        slots = [jnp.where(place == p, j, slots[p]) for p in range(ROWS_DEV)]
        free_before = free_before + early
    return slots, places


def with_row(block, position, row):
    rows = lax.broadcasted_iota(jnp.int32, block.shape, 0)
    return jnp.where(rows == position, jnp.broadcast_to(row, block.shape), block)


def attend(query_rows, keys, live):
    scores = dot_rows(query_rows, keys[...]) * (HD + ROPE) ** (-0.5)
    positions = lax.broadcasted_iota(jnp.int32, scores.shape, 1)
    scores = jnp.where(positions < live, scores, -1e30)
    powers = jnp.exp(scores - jnp.max(scores, axis=1, keepdims=True))
    weights = (powers / jnp.sum(powers, axis=1, keepdims=True)).astype(jnp.bfloat16)
    return jnp.dot(weights, keys[:, :KVR], preferred_element_type=jnp.float32)


def fresh_keys(latent, positions):
    content = latent[:, :KVR]
    content = content * lax.rsqrt(jnp.mean(content * content, axis=1, keepdims=True) + epsilon)
    rotary = latent[:, KVR:]
    lane = lax.broadcasted_iota(jnp.int32, rotary.shape, 1)
    half = ROPE // 2
    power = lax.rem(lane, half).astype(jnp.float32) * (-2.0 / ROPE * math.log(10000.0))
    angles = positions.astype(jnp.float32) * jnp.exp(power)
    turned = jnp.where(lane < half, -pltpu.roll(rotary, 128 - half, 1), pltpu.roll(rotary, half, 1))
    return content, rotary * jnp.cos(angles) + turned * jnp.sin(angles)


def enter(here, barrier):
    devices = [here.on_ring(1), here.on_ring(-1), here.on_core()]
    for o in range(1, N):
        devices += [here.on_x(lax.rem(here.x + o, N)), here.on_chip(*here.chip(o)), here.on_chip(*here.chip(o * N))]
    for device in devices:
        pl.semaphore_signal(barrier, inc=1, device_id=device, device_id_type=MESH)
    return len(devices)


def tell(here, sem, line):
    for device in known_line(here, line):
        pl.semaphore_signal(sem, inc=1, device_id=device, device_id_type=MESH)


def hear(here, sem, line):
    pl.semaphore_wait(sem, len(known_line(here, line)))


def known_line(here, line):
    if line == "core":
        return [here.on_core()]
    if line == "x":
        return [here.on_x(lax.rem(here.x + o, N)) for o in range(1, N)]
    return [here.on_chip(*here.chip(o * N)) for o in range(1, N)]


def head_copy(here, r, step, i):
    place = here.c * BLOCKS + here.y * N + here.z
    k = lax.rem(here.z * 2 + here.c + i // N, 2 * N)
    x = lax.rem(here.x + i, N)
    kept = (x == here.x) & (here.x * (2 * N) + k == here.me)

    def copy():
        return remote(
            r.heads.at[step, k],
            r.head_rows.at[step, place],
            r.head_send.at[step, i],
            r.head_recv.at[step],
            {"dp": here.x * (2 * N) + k, "tp": x},
        )

    def local():
        return pltpu.make_async_copy(
            r.heads.at[step, k], r.head_rows.at[step, place], r.head_recv.at[step]
        )

    return kept, copy, local


def keep(r, line, row, result):
    for c in range(KVR // 128):
        r.head_latent[line, c, row * HEADS : (row + 1) * HEADS, :] = result[:, c * 128 : (c + 1) * 128]


def value_up(here, r, line):
    def head(h):
        rows = jnp.concatenate(
            [r.head_latent.at[line, c][pl.ds(h, ROWS_DEV, stride=HEADS), :] for c in range(KVR // 128)], axis=1
        ).astype(jnp.bfloat16)
        return jnp.dot(rows, r.vup[h], preferred_element_type=jnp.float32)

    for h in range(0, HEADS, 2):
        r.heads[line, h // N, h % N // 2] = jnp.concatenate([head(h), head(h + 1)], axis=0).astype(jnp.bfloat16)

    @pl.loop(0, GROUPS)
    def _(i):
        kept, copy, local = head_copy(here, r, line, i)

        @pl.when(kept)
        def _():
            local().start()

        @pl.when(jnp.logical_not(kept))
        def _():
            copy().start()


def front_line(here, r):
    loads = {}
    for i, (name, src, dst) in enumerate(
        (
            ("lw", r.lw_hbm, r.lw),
            ("queries", r.queries_hbm, r.queries),
            ("vup", r.vup_hbm, r.vup),
            ("wo", r.wo_hbm, r.wo),
            ("wg", r.wg_hbm, r.wg.at[pl.ds(0, FF_DEV)]),
            ("wu", r.wu_hbm, r.wu),
            ("wd", r.wd_hbm, r.wd),
        )
    ):
        loads[name] = pltpu.make_async_copy(src, dst, r.load_sem.at[i])
    r.loads = loads
    slot_loads = [
        pltpu.make_async_copy(r.cache_hbm.at[j], r.cache.at[j], r.cache_sem.at[j]) for j in range(ROWS_DEV)
    ]
    for load in slot_loads:
        load.start()
    loads["lw"].start()
    barrier = pltpu.get_barrier_semaphore()
    entered = enter(here, barrier)

    moves, me = r.moves, here.me
    a0, b0, a1, b1 = moves[0, 0, me], moves[0, 1, me], moves[1, 0, me], moves[1, 1, me]
    slots, places = slot_order(moves, me)
    r.slots, r.places = slots, places
    r.wg[pl.ds(FF_DEV, SPARE), :] = jnp.zeros((SPARE, WIDTH), jnp.bfloat16)
    wide = r.tokens[...].astype(jnp.float32)
    r.tokens_wide[...] = wide
    r.latents[...] = jnp.zeros_like(r.latents)
    r.latents[:, LAT + 64 :] = jnp.broadcast_to(jnp.sum(wide * wide, axis=1, keepdims=True), (OWN, 128))

    def move(leaving, arrived, sem, part):
        rows = pl.ds(part * MOVE_ROWS, MOVE_ROWS)
        return [
            send(
                leaving.at[i, rows],
                arrived.at[i, rows],
                sem.at[0, i, part],
                sem.at[1, i, part],
                here.on_ring(o),
            )
            for i, o in enumerate((1, -1))
        ]

    for load in slot_loads:
        load.wait()
    r.leaving0[0] = r.cache[a0]
    r.leaving0[1] = r.cache[b0]
    pl.semaphore_wait(barrier, entered)
    tell(here, r.y_in, "y")
    moving0 = [move(r.leaving0, r.arrived0, r.move0_sem, part) for part in range(MOVE_PARTS)]

    loads["lw"].wait()
    r.latents[:, :LAT] = dot_rows(r.tokens[...], r.lw[...])
    copies = [
        send(
            r.latents,
            r.latent_rows.at[o - 1],
            r.latent_sem.at[0, o - 1],
            r.latent_sem.at[1, o - 1],
            here.on_x(lax.rem(here.x + o, N)),
        )
        for o in FAR_FIRST
    ]
    for name in ("queries", "vup", "wo", "wg", "wu", "wd"):
        loads[name].start()
    held = [held_first(r.lengths, moves, me, j) for j in range(ROWS_DEV)]
    held += [held_second(r.lengths, moves, me, j) for j in range(ROWS_DEV)]
    row = lax.broadcasted_iota(jnp.int32, (OWN, 128), 0)
    positions = jnp.zeros((OWN, 128), jnp.int32)
    for i in range(OWN):
        positions = jnp.where(row == i, held[i], positions)

    def held_at(step, place):
        result = held[step * ROWS_DEV]
        for j in range(1, ROWS_DEV):
            result = jnp.where(slots[place] == j, held[step * ROWS_DEV + j], result)
        return result

    held_by_place = [[held_at(step, p) for p in range(ROWS_DEV)] for step in range(STEPS)]
    yield
    hear(here, r.y_in, "y")
    tell(here, r.x_in, "x")
    for copy in copies:
        copy.wait()
    total = r.latents[...]
    for o in range(N - 1):
        total = total + r.latent_rows[o]
    scale = lax.rsqrt(total[:, LAT + 64 :] / D + epsilon)[:, :1]
    content, rotary = fresh_keys(total[:, : LAT + 64] * scale, positions)
    r.fresh[:, :KVR] = content
    r.fresh[:, KVR:] = rotary

    def fresh_row(step, place):
        return r.fresh[pl.ds(step * ROWS_DEV + slots[place], 1), :LAT].astype(jnp.bfloat16)

    loads["queries"].wait()
    r.ordered_copies = []

    def put_out(ref, place):
        copy = pltpu.make_async_copy(ref, r.ordered.at[place], r.out_sem.at[place])
        copy.start()
        r.ordered_copies.append(copy)

    for p in range(EARLY):
        first, second = held_by_place[0][p], held_by_place[1][p]
        block = with_row(r.cache[slots[p]], first, fresh_row(0, p))
        r.early_keys[p] = with_row(block, second, fresh_row(1, p))
        put_out(r.early_keys.at[p], p)
        rows = jnp.concatenate([r.queries[0, slots[p]], r.queries[1, slots[p]]], axis=0)
        step_row = lax.broadcasted_iota(jnp.int32, (2 * HEADS, 1), 0)
        live = jnp.where(step_row < HEADS, first + 1, second + 1)
        result = attend(rows, r.early_keys.at[p], live)
        keep(r, 0, p, result[:HEADS])
        keep(r, 0, EARLY + p, result[HEADS:])

    yield
    hear(here, r.x_in, "x")
    tell(here, r.core_in, "core")
    place_a, place_b = 0, 0
    for p in range(EARLY, ROWS_DEV):
        place_a = jnp.where(slots[p] == a1, p - EARLY, place_a)
        place_b = jnp.where(slots[p] == b1, p - EARLY, place_b)

    def arrive(step, keys, part, arrived, own_a, own_b, kept):
        rows = pl.ds(part * MOVE_ROWS, MOVE_ROWS)
        for p in range(EARLY, ROWS_DEV):
            block = jnp.where(
                slots[p] == own_a,
                arrived[1, rows],
                jnp.where(slots[p] == own_b, arrived[0, rows], kept(p, rows)),
            )
            keys[p - EARLY, rows] = with_row(
                block, held_by_place[step][p] - part * MOVE_ROWS, fresh_row(step, p)
            )

    moving1 = []
    for part in range(MOVE_PARTS):
        rows = pl.ds(part * MOVE_ROWS, MOVE_ROWS)
        for copy in moving0[part]:
            copy.wait()
        arrive(0, r.keys0, part, r.arrived0, a0, b0, lambda p, rows: r.cache[slots[p], rows])
        r.leaving1[0, rows] = r.keys0[place_a, rows]
        r.leaving1[1, rows] = r.keys0[place_b, rows]
        moving1.append(move(r.leaving1, r.arrived1, r.move1_sem, part))
    yield
    loads["vup"].wait()
    hear(here, r.core_in, "core")
    value_up(here, r, 0)
    yield
    for p in range(EARLY, ROWS_DEV):
        keep(
            r, 1, p - EARLY,
            attend(r.queries[0, slots[p]], r.keys0.at[p - EARLY], held_by_place[0][p] + 1),
        )

    yield
    for part in range(MOVE_PARTS):
        for copy in moving1[part]:
            copy.wait()
        arrive(1, r.keys1, part, r.arrived1, a1, b1, lambda p, rows: r.keys0[p - EARLY, rows])
    for p in range(EARLY, ROWS_DEV):
        put_out(r.keys1.at[p - EARLY], p)
        keep(
            r, 1, p,
            attend(r.queries[1, slots[p]], r.keys1.at[p - EARLY], held_by_place[1][p] + 1),
        )
    yield
    value_up(here, r, 1)
    yield


def reduce_over_groups(here, r, step, use):
    own, peer = r.own.at[step], r.peer_rows.at[use, step]
    sem = r.sum_sem.at[use, step]
    sums, rows = r.sums.at[step], r.rows.at[use, step]
    r.core_copy[use, step].wait()
    copies = {}
    for o in reversed(CHIPS):
        y, z = here.chip(o)
        k = y * N + z
        sums[k] = (own[k].astype(jnp.float32) + peer[k].astype(jnp.float32)).astype(jnp.bfloat16)
        copies[o] = send(sums.at[k], rows.at[o], sem.at[0, o], sem.at[1, o], here.on_chip(y, z))
    k = here.y * N + here.z
    total = own[k].astype(jnp.float32) + peer[k].astype(jnp.float32)
    yield
    for o in CHIPS:
        copies[o].wait()
        total = total + rows[o].astype(jnp.float32)
    return total


def project_both(here, r, step, use, lhs, weight):
    project(lhs(1 - here.c), weight, r.to_peer.at[step])
    core_sem = r.core_sem.at[use, step]
    r.core_copy[use, step] = send(
        r.to_peer.at[step], r.peer_rows.at[use, step], core_sem.at[0], core_sem.at[1], here.on_core()
    )
    project(lhs(here.c), weight, r.own.at[step])


def back_line(here, r, step):
    f32, bf16 = jnp.float32, jnp.bfloat16

    pltpu.make_async_copy(r.head_rows.at[step], r.head_rows.at[step], r.head_recv.at[step]).wait()
    rows = r.head_rows[step].astype(f32)
    for h in range(N):
        first = h % 2 * ROWS_DEV
        r.head_block[:, h * HD : (h + 1) * HD] = (
            rows[:, h // 2, first : first + ROWS_DEV].reshape(2 * HALF, HD).astype(bf16)
        )
    if step == 0:
        r.loads["wo"].wait()

    def half(ref, c):
        return ref[pl.ds(pl.multiple_of(c * HALF, HALF), HALF), :]

    project_both(here, r, step, 0, lambda c: half(r.head_block, c), r.wo[...])
    for i in range(ROWS_DEV):
        token = i // EARLY * ROWS_DEV + r.slots[step * EARLY + i % EARLY]
        r.line_tokens[step, i : i + 1, :] = r.tokens_wide[pl.ds(token, 1), :]
    r.mixed[step] = stacked(r.line_tokens[step])[0]
    yield
    attention = yield from reduce_over_groups(here, r, step, 0)
    mixed = (r.mixed[step] + attention).astype(bf16).astype(f32)
    r.mixed[step] = mixed

    mixed_all = r.mixed_all.at[step]
    mine = mixed_all.at[here.c, here.y, here.z]
    mine[...] = mixed.astype(bf16)
    sem, core_sem = r.gather_sem.at[step], r.gather_core.at[step]
    copies = {}
    for o in reversed(CHIPS):
        copies[o] = send(mine, mine, sem.at[0, o], sem.at[1, o], here.on_chip(*here.chip(o)))

    @pl.loop(0, GROUPS)
    def _(i):
        kept, copy, _ = head_copy(here, r, step, i)

        @pl.when(jnp.logical_not(kept))
        def _():
            copy().wait_send()

    yield
    handed = []
    for o in (0, *NEAR_FIRST):
        for i in range(N):
            if o + i:
                copies[o * N + i].wait()
        block = mixed_all.at[here.c, lax.rem(here.y + N - o, N)]
        handed.append(send(block, block, core_sem.at[0, o], core_sem.at[1, o], here.on_core()))

    if step == 0:
        r.loads["wg"].wait()
        r.loads["wu"].wait()
    sums = (
        (r.gate_part.at[step], r.gate_rows.at[step], r.gate_sem.at[step], r.wg),
        (r.up_part.at[step], r.up_rows.at[step], r.up_sem.at[step], r.wu),
    )

    def chunk_copy(part, rows, sem, k):
        slot = lax.rem(k - here.x + N, N) - 1
        return remote(part.at[k], rows.at[slot], sem.at[0, slot], sem.at[1, slot], here.on_x(k))

    for core in (here.c, 1 - here.c):
        if core is not here.c:
            yield
            for copy in handed:
                copy.wait()
        wide = unstacked(mixed_all[core].astype(f32).reshape(BLOCKS, TILE, COLS))
        r.lhs[...] = (wide * r.gain[...].reshape(1, WIDTH)).astype(bf16)
        pieces = in_pieces(jnp.sum(wide * wide, axis=1, keepdims=True))
        for part, rows, sem, weight in sums:
            result = dot_rows(r.lhs[...], weight[...])
            if weight is r.wg:
                lane = lax.broadcasted_iota(jnp.int32, result.shape, 1)
                for i, piece in enumerate(pieces):
                    result = jnp.where(lane == FF_DEV + i, piece, result)
            part[pl.ds(2 * core, 2)] = result.astype(bf16).reshape(2, CHUNK, -1)
            for i in range(2):
                k = 2 * core + lax.rem(here.x + i, 2)

                @pl.when(k != here.x)
                def _():
                    chunk_copy(part, rows, sem, k).start()

    yield
    totals = []
    for part, rows, sem, _ in sums:
        total = part[here.x].astype(f32)
        for o in NEAR_FIRST:
            chunk_copy(part, rows, sem, lax.rem(here.x + o, N)).wait()
        for o in range(N - 1):
            total = total + rows[o].astype(f32)
        totals.append(total)
    gate, up = totals
    lane = lax.broadcasted_iota(jnp.int32, gate.shape, 1)
    squares = jnp.sum(jnp.where(lane >= FF_DEV, gate, 0.0), axis=1, keepdims=True)
    scale = lax.rsqrt(squares / D + epsilon)
    gate, up = gate[:, :FF_DEV] * scale, up * scale
    activation = r.activation.at[step]
    activation[here.x] = (gate / (1.0 + jnp.exp(-gate)) * up).astype(bf16)
    mine = activation.at[here.x]
    sem = r.act_sem.at[step]
    copies = {}
    for o in FAR_FIRST:
        x = lax.rem(here.x + o, N)
        copies[o] = send(mine, mine, sem.at[0, o - 1], sem.at[1, o - 1], here.on_x(x))
    yield
    for o in NEAR_FIRST:
        copies[o].wait()

    if step == 0:
        r.loads["wd"].wait()
    project_both(
        here, r, step, 1, lambda c: activation[pl.ds(2 * c, 2)].reshape(HALF, FF_DEV), r.wd[...]
    )
    yield
    down = yield from reduce_over_groups(here, r, step, 1)
    r.results[step * ROWS_DEV : (step + 1) * ROWS_DEV, :] = unstacked((r.mixed[step] + down)[None])
    yield


ORDER = "FFFFF00FF0110010110010111"

INPUTS = (
    "lengths", "moves", "tokens", "gain", "lw_hbm", "queries_hbm", "cache_hbm", "vup_hbm",
    "wo_hbm", "wg_hbm", "wu_hbm", "wd_hbm",
)


def layer_kernel(names, *refs):
    r = types.SimpleNamespace(**dict(zip(names, refs)))
    r.core_copy = {}
    here = Place()
    lines = {"F": front_line(here, r), "0": back_line(here, r, 0), "1": back_line(here, r, 1)}
    for name in ORDER:
        next(lines[name], None)
    for i in range(OWN):
        place = r.places[i % ROWS_DEV]
        row = place // EARLY * ROWS_DEV + i // ROWS_DEV * EARLY + lax.rem(place, EARLY)
        r.sorted_results[i : i + 1, :] = r.results[pl.ds(row, 1), :]
    r.out[...] = r.sorted_results[...].astype(jnp.bfloat16)
    for copy in r.ordered_copies:
        copy.wait()


def layer(lengths, moves, tokens, gain, lw, queries, cache, vup, wo, wg, wu, wd):
    bf16, f32 = jnp.bfloat16, jnp.float32
    vmem = pl.BlockSpec(memory_space=pltpu.VMEM)
    smem = pl.BlockSpec(memory_space=pltpu.SMEM)
    hbm = pl.BlockSpec(memory_space=pl.ANY)
    slot = cache.shape[1:]

    def dma(*shape):
        return pltpu.SemaphoreType.DMA(shape)

    def held(*shape, dtype=bf16):
        return pltpu.VMEM(shape, dtype)

    scratch = dict(
        cache=held(*cache.shape),
        lw=held(*lw.shape),
        queries=held(*queries.shape),
        vup=held(*vup.shape),
        wo=held(*wo.shape),
        wg=held(FF_DEV + SPARE, WIDTH),
        wu=held(*wu.shape),
        wd=held(*wd.shape),
        latents=held(OWN, LAT + 64 + 128, dtype=f32),
        latent_rows=held(N - 1, OWN, LAT + 64 + 128, dtype=f32),
        fresh=held(OWN, LAT + 64, dtype=f32),
        leaving0=held(2, *slot),
        leaving1=held(2, *slot),
        arrived0=held(2, *slot),
        arrived1=held(2, *slot),
        early_keys=held(EARLY, *slot),
        keys0=held(ROWS_DEV - EARLY, *slot),
        keys1=held(ROWS_DEV - EARLY, *slot),
        head_latent=held(2, KVR // 128, ROWS_DEV * HEADS, 128, dtype=f32),
        heads=held(STEPS, 2 * N, N // 2, TILE, HD),
        head_rows=held(STEPS, GROUPS, N // 2, TILE, HD),
        head_block=held(2 * HALF, N * HD),
        to_peer=held(STEPS, BLOCKS, TILE, COLS),
        own=held(STEPS, BLOCKS, TILE, COLS),
        peer_rows=held(2, STEPS, BLOCKS, TILE, COLS),
        sums=held(STEPS, BLOCKS, TILE, COLS),
        rows=held(2, STEPS, BLOCKS, TILE, COLS),
        mixed=held(STEPS, TILE, COLS, dtype=f32),
        mixed_all=held(STEPS, 2, N, N, TILE, COLS),
        lhs=held(HALF, WIDTH),
        gate_part=held(STEPS, N, CHUNK, FF_DEV + SPARE),
        up_part=held(STEPS, N, CHUNK, FF_DEV),
        gate_rows=held(STEPS, N - 1, CHUNK, FF_DEV + SPARE),
        up_rows=held(STEPS, N - 1, CHUNK, FF_DEV),
        activation=held(STEPS, N, CHUNK, FF_DEV),
        results=held(OWN, WIDTH, dtype=f32),
        sorted_results=held(OWN, WIDTH, dtype=f32),
        tokens_wide=held(OWN, WIDTH, dtype=f32),
        line_tokens=held(2, ROWS_DEV, WIDTH, dtype=f32),
        y_in=pltpu.SemaphoreType.REGULAR,
        x_in=pltpu.SemaphoreType.REGULAR,
        core_in=pltpu.SemaphoreType.REGULAR,
        load_sem=dma(7),
        cache_sem=dma(ROWS_DEV),
        latent_sem=dma(2, N - 1),
        move0_sem=dma(2, 2, MOVE_PARTS),
        move1_sem=dma(2, 2, MOVE_PARTS),
        out_sem=dma(ROWS_DEV),
        head_send=dma(STEPS, GROUPS),
        head_recv=dma(STEPS),
        core_sem=dma(2, STEPS, 2),
        sum_sem=dma(2, STEPS, 2, BLOCKS),
        gather_sem=dma(STEPS, 2, BLOCKS),
        gather_core=dma(STEPS, 2, N),
        gate_sem=dma(STEPS, 2, N - 1),
        up_sem=dma(STEPS, 2, N - 1),
        act_sem=dma(STEPS, 2, N - 1),
    )
    names = (*INPUTS, "out", "ordered", *scratch)

    def kernel(*refs):
        layer_kernel(names, *refs)

    return pl.pallas_call(
        kernel,
        out_shape=(
            jax.ShapeDtypeStruct((OWN, WIDTH), bf16),
            jax.ShapeDtypeStruct(cache.shape, bf16),
        ),
        in_specs=[smem, smem, vmem, vmem] + [hbm] * 8,
        out_specs=(vmem, hbm),
        scratch_shapes=list(scratch.values()),
        compiler_params=pltpu.CompilerParams(
            collective_id=0, has_side_effects=True, vmem_limit_bytes=58 * 1024 * 1024
        ),
        name="layer",
    )(lengths, moves, tokens, gain, lw, queries, cache, vup, wo, wg, wu, wd)


def finish_kernel(
    lengths, moves, group, ordered, rows, final_cache, final_rows, final_lengths, moved, slots, row_block, sems, row_sem
):
    _, places = slot_order(moves, group[0])
    loads = [pltpu.make_async_copy(ordered.at[places[j]], slots.at[j], sems.at[0, j]) for j in range(ROWS_DEV)]
    stores = [pltpu.make_async_copy(slots.at[j], final_cache.at[j], sems.at[1, j]) for j in range(ROWS_DEV)]
    loads.append(pltpu.make_async_copy(rows, row_block, row_sem.at[0]))
    stores.append(pltpu.make_async_copy(row_block, final_rows, row_sem.at[1]))
    for load in loads:
        load.start()

    def pass_on(first, last):
        for load, store in zip(loads[first:last], stores[first:last]):
            load.wait()
            store.start()

    @pl.loop(0, GROUPS)
    def _(g):
        for j in range(ROWS_DEV):
            moved[g * ROWS_DEV + j] = lengths[g * ROWS_DEV + j] + 1

    pass_on(0, 3)

    @pl.loop(0, GROUPS)
    def _(g):
        right = lax.rem(g + 1, GROUPS)
        left = lax.rem(g + GROUPS - 1, GROUPS)
        moved[g * ROWS_DEV + moves[0, 0, g]] = lengths[right * ROWS_DEV + moves[0, 1, right]] + 1
        moved[g * ROWS_DEV + moves[0, 1, g]] = lengths[left * ROWS_DEV + moves[0, 0, left]] + 1

    pass_on(3, ROWS_DEV + 1)

    @pl.loop(0, GROUPS)
    def _(g):
        for j in range(ROWS_DEV):
            final_lengths[g * ROWS_DEV + j] = moved[g * ROWS_DEV + j] + 1

    @pl.loop(0, GROUPS)
    def _(g):
        right = lax.rem(g + 1, GROUPS)
        left = lax.rem(g + GROUPS - 1, GROUPS)
        final_lengths[g * ROWS_DEV + moves[1, 0, g]] = moved[right * ROWS_DEV + moves[1, 1, right]] + 1
        final_lengths[g * ROWS_DEV + moves[1, 1, g]] = moved[left * ROWS_DEV + moves[1, 0, left]] + 1

    for store in stores:
        store.wait()


def finish(lengths, moves, group, ordered, rows):
    smem = pl.BlockSpec(memory_space=pltpu.SMEM)
    hbm = pl.BlockSpec(memory_space=pltpu.HBM)
    return pl.pallas_call(
        finish_kernel,
        out_shape=(
            jax.ShapeDtypeStruct(ordered.shape, ordered.dtype),
            jax.ShapeDtypeStruct(rows.shape, rows.dtype),
            jax.ShapeDtypeStruct(lengths.shape, jnp.int32),
        ),
        in_specs=[smem, smem, smem, hbm, hbm],
        out_specs=(hbm, hbm, smem),
        scratch_shapes=[
            pltpu.SMEM(lengths.shape, jnp.int32),
            pltpu.VMEM(ordered.shape, ordered.dtype),
            pltpu.VMEM(rows.shape, rows.dtype),
            pltpu.SemaphoreType.DMA((2, ROWS_DEV)),
            pltpu.SemaphoreType.DMA((2,)),
        ],
        compiler_params=pltpu.CompilerParams(vmem_limit_bytes=60 * 1024 * 1024),
        name="finish",
    )(lengths, moves, group, ordered, rows)


def on_device(
    latent_cache,
    lengths,
    slot_moves,
    hidden_in,
    queries,
    latent_weight,
    value_up_projection,
    out_weight,
    post_gain,
    gate_projection_matrix,
    up_weight,
    down_weight,
):
    moves = jnp.swapaxes(slot_moves, 1, 2)
    rows, ordered = layer(
        lengths,
        moves,
        hidden_in.reshape(OWN, WIDTH),
        post_gain,
        latent_weight.T,
        queries,
        latent_cache,
        value_up_projection,
        out_weight,
        gate_projection_matrix.T,
        up_weight.T,
        down_weight,
    )
    group = lax.axis_index("dp").reshape(1)
    final_cache, final_rows, final_lengths = finish(lengths, moves, group, ordered, rows)
    return (final_rows.reshape(STEPS, ROWS_DEV, WIDTH), final_cache, final_lengths)


def solution(mesh):
    return jax.shard_map(
        on_device,
        mesh=mesh,
        in_specs=(
            P("dp", None, None),
            P(),
            P(),
            P(None, "dp", "tp"),
            P(None, "dp", "tp", None),
            P("tp", None),
            P("tp", None, None),
            P("dp", "tp"),
            P("tp"),
            P("tp", "dp"),
            P("tp", "dp"),
            P("dp", "tp"),
        ),
        out_specs=(P(None, "dp", "tp"), P("dp", None, None), P()),
        check_vma=False,
    )
```

```python
import math
import types

import jax
import jax.numpy as jnp
from jax import lax
from jax.experimental import pallas as pl
from jax.experimental.pallas import tpu as pltpu
from jax.sharding import PartitionSpec as P

D = 7168
KVR = 512
ROPE = 64
HD = 128
STEPS = 2
ROWS_DEV = 8
N = 4
OWN = STEPS * ROWS_DEV
BLOCKS = N * N
HALF = BLOCKS * ROWS_DEV
WIDTH = D // N
COLS = WIDTH // 2
TILE = 2 * ROWS_DEV
FF_DEV = 576
CHUNK = 2 * HALF // N
HEADS = 32
LAT = KVR + ROPE
GROUPS = 2 * N * N
EARLY = 4
CAP = 448
MOVE_PARTS = 4
MOVE_ROWS = CAP // MOVE_PARTS
NEAR_FIRST = (1, 3, 2)
FAR_FIRST = (2, 1, 3)
HOPS = (0, 1, 2, 1)
CHIPS = sorted(range(1, N * N), key=lambda o: HOPS[o // N] + HOPS[o % N])
SPARE = 64
MESH = pl.DeviceIdType.MESH


epsilon = 1e-06


def dot_rows(lhs, rhs):
    return lax.dot_general(
        lhs, rhs, (((1,), (1,)), ((), ())), preferred_element_type=jnp.float32
    )


class Place:
    def __init__(self):
        dp = lax.axis_index("dp")
        self.x = lax.axis_index("tp")
        self.y = dp // (2 * N)
        self.z = (dp // 2) % N
        self.c = dp % 2
        self.me = dp

    def on_chip(self, y, z):
        return {"dp": y * (2 * N) + z * 2 + self.c, "tp": self.x}

    def on_core(self):
        return {"dp": self.me + 1 - 2 * self.c, "tp": self.x}

    def on_x(self, k):
        return {"dp": self.me, "tp": k}

    def on_ring(self, o):
        return {"dp": lax.rem(self.me + o + GROUPS, GROUPS), "tp": self.x}

    def chip(self, offset):
        return lax.rem(self.y + offset // N, N), lax.rem(self.z + offset % N, N)


def remote(src, dst, send_sem, recv_sem, device):
    return pltpu.make_async_remote_copy(
        src_ref=src,
        dst_ref=dst,
        send_sem=send_sem,
        recv_sem=recv_sem,
        device_id=device,
        device_id_type=MESH,
    )


def send(*args):
    copy = remote(*args)
    copy.start()
    return copy


def wait_all(block, sem):
    pltpu.make_async_copy(block, block, sem).wait()


def stacked(rows):
    left = rows[:, :COLS].reshape(-1, ROWS_DEV, COLS)
    right = rows[:, COLS:].reshape(-1, ROWS_DEV, COLS)
    return jnp.concatenate([left, right], axis=1)


def unstacked(blocks):
    left = blocks[:, :ROWS_DEV].reshape(-1, COLS)
    right = blocks[:, ROWS_DEV:].reshape(-1, COLS)
    return jnp.concatenate([left, right], axis=1)


def project(lhs, weight, out):
    for start in range(0, COLS, 256):
        width = min(256, COLS - start)
        parts = [
            jnp.dot(
                lhs, weight[:, first + start : first + start + width], preferred_element_type=jnp.float32
            ).reshape(-1, ROWS_DEV, width)
            for first in (0, COLS)
        ]
        out[:, :, start : start + width] = jnp.concatenate(parts, axis=1).astype(jnp.bfloat16)


def in_pieces(value):
    pieces = []
    for _ in range(3):
        piece = value.astype(jnp.bfloat16).astype(jnp.float32)
        pieces.append(piece)
        value = value - piece
    return pieces


def source_of(moves, step, group, slot):
    right = lax.rem(group + 1, GROUPS)
    left = lax.rem(group + GROUPS - 1, GROUPS)
    to_right = slot == moves[step, 0, group]
    to_left = slot == moves[step, 1, group]
    source_group = jnp.where(to_right, right, jnp.where(to_left, left, group))
    source_slot = jnp.where(
        to_right, moves[step, 1, right], jnp.where(to_left, moves[step, 0, left], slot)
    )
    return source_group, source_slot


def held_first(lengths, moves, group, slot):
    source_group, source_slot = source_of(moves, 0, group, slot)
    return lengths[source_group * ROWS_DEV + source_slot]


def held_second(lengths, moves, group, slot):
    source_group, source_slot = source_of(moves, 1, group, slot)
    return held_first(lengths, moves, source_group, source_slot) + 1


def slot_order(moves, group):
    free_before, slots, places = 0, [0] * ROWS_DEV, []
    for j in range(ROWS_DEV):
        moved = (
            (j == moves[0, 0, group])
            | (j == moves[0, 1, group])
            | (j == moves[1, 0, group])
            | (j == moves[1, 1, group])
        )
        early = jnp.where(moved | (free_before >= EARLY), 0, 1)
        place = jnp.where(early == 1, free_before, EARLY + j - free_before)
        places.append(place)
        slots = [jnp.where(place == p, j, slots[p]) for p in range(ROWS_DEV)]
        free_before = free_before + early
    return slots, places


def with_row(block, position, row):
    rows = lax.broadcasted_iota(jnp.int32, block.shape, 0)
    return jnp.where(rows == position, jnp.broadcast_to(row, block.shape), block)


def attend(query_rows, keys, live):
    scores = dot_rows(query_rows, keys[...]) * (HD + ROPE) ** (-0.5)
    positions = lax.broadcasted_iota(jnp.int32, scores.shape, 1)
    scores = jnp.where(positions < live, scores, -1e30)
    powers = jnp.exp(scores - jnp.max(scores, axis=1, keepdims=True))
    weights = (powers / jnp.sum(powers, axis=1, keepdims=True)).astype(jnp.bfloat16)
    return jnp.dot(weights, keys[:, :KVR], preferred_element_type=jnp.float32)


def fresh_keys(latent, positions):
    content = latent[:, :KVR]
    content = content * lax.rsqrt(jnp.mean(content * content, axis=1, keepdims=True) + epsilon)
    rotary = latent[:, KVR:]
    lane = lax.broadcasted_iota(jnp.int32, rotary.shape, 1)
    half = ROPE // 2
    power = lax.rem(lane, half).astype(jnp.float32) * (-2.0 / ROPE * math.log(10000.0))
    angles = positions.astype(jnp.float32) * jnp.exp(power)
    turned = jnp.where(lane < half, -pltpu.roll(rotary, 128 - half, 1), pltpu.roll(rotary, half, 1))
    return content, rotary * jnp.cos(angles) + turned * jnp.sin(angles)


def enter(here, barrier):
    devices = [here.on_ring(1), here.on_ring(-1), here.on_core()]
    for o in range(1, N):
        devices += [here.on_x(lax.rem(here.x + o, N)), here.on_chip(*here.chip(o)), here.on_chip(*here.chip(o * N))]
    for device in devices:
        pl.semaphore_signal(barrier, inc=1, device_id=device, device_id_type=MESH)
    return len(devices)


def tell(here, sem, line):
    for device in known_line(here, line):
        pl.semaphore_signal(sem, inc=1, device_id=device, device_id_type=MESH)


def hear(here, sem, line):
    pl.semaphore_wait(sem, len(known_line(here, line)))


def known_line(here, line):
    if line == "core":
        return [here.on_core()]
    if line == "x":
        return [here.on_x(lax.rem(here.x + o, N)) for o in range(1, N)]
    return [here.on_chip(*here.chip(o * N)) for o in range(1, N)]


def head_copy(here, r, step, i):
    place = here.c * BLOCKS + here.y * N + here.z
    k = lax.rem(here.z * 2 + here.c + i // N, 2 * N)
    x = lax.rem(here.x + i, N)
    kept = (x == here.x) & (here.x * (2 * N) + k == here.me)

    def copy():
        return remote(
            r.heads.at[step, k],
            r.head_rows.at[step, place],
            r.head_send.at[step, i],
            r.head_recv.at[step],
            {"dp": here.x * (2 * N) + k, "tp": x},
        )

    def local():
        return pltpu.make_async_copy(
            r.heads.at[step, k], r.head_rows.at[step, place], r.head_recv.at[step]
        )

    return kept, copy, local


def keep(r, line, row, result):
    for c in range(KVR // 128):
        r.head_latent[line, c, row * HEADS : (row + 1) * HEADS, :] = result[:, c * 128 : (c + 1) * 128]


def value_up(here, r, line):
    def head(h):
        rows = jnp.concatenate(
            [r.head_latent.at[line, c][pl.ds(h, ROWS_DEV, stride=HEADS), :] for c in range(KVR // 128)], axis=1
        ).astype(jnp.bfloat16)
        return jnp.dot(rows, r.vup[h], preferred_element_type=jnp.float32)

    for h in range(0, HEADS, 2):
        r.heads[line, h // N, h % N // 2] = jnp.concatenate([head(h), head(h + 1)], axis=0).astype(jnp.bfloat16)

    @pl.loop(0, GROUPS)
    def _(i):
        kept, copy, local = head_copy(here, r, line, i)

        @pl.when(kept)
        def _():
            local().start()

        @pl.when(jnp.logical_not(kept))
        def _():
            copy().start()


def front_line(here, r):
    loads = {}
    for i, (name, src, dst) in enumerate(
        (
            ("lw", r.lw_hbm, r.lw),
            ("queries", r.queries_hbm, r.queries),
            ("vup", r.vup_hbm, r.vup),
            ("wo", r.wo_hbm, r.wo),
            ("wg", r.wg_hbm, r.wg.at[pl.ds(0, FF_DEV)]),
            ("wu", r.wu_hbm, r.wu),
            ("wd", r.wd_hbm, r.wd),
        )
    ):
        loads[name] = pltpu.make_async_copy(src, dst, r.load_sem.at[i])
    r.loads = loads
    slot_loads = [
        pltpu.make_async_copy(r.cache_hbm.at[j], r.cache.at[j], r.cache_sem.at[j]) for j in range(ROWS_DEV)
    ]
    for load in slot_loads:
        load.start()
    loads["lw"].start()
    barrier = pltpu.get_barrier_semaphore()
    entered = enter(here, barrier)

    moves, me = r.moves, here.me
    a0, b0, a1, b1 = moves[0, 0, me], moves[0, 1, me], moves[1, 0, me], moves[1, 1, me]
    slots, places = slot_order(moves, me)
    r.slots, r.places = slots, places
    r.wg[pl.ds(FF_DEV, SPARE), :] = jnp.zeros((SPARE, WIDTH), jnp.bfloat16)
    wide = r.tokens[...].astype(jnp.float32)
    r.tokens_wide[...] = wide
    r.latents[...] = jnp.zeros_like(r.latents)
    r.latents[:, LAT + 64 :] = jnp.broadcast_to(jnp.sum(wide * wide, axis=1, keepdims=True), (OWN, 128))

    def move(leaving, arrived, sem, part):
        rows = pl.ds(part * MOVE_ROWS, MOVE_ROWS)
        return [
            send(
                leaving.at[i, rows],
                arrived.at[i, rows],
                sem.at[0, i, part],
                sem.at[1, i, part],
                here.on_ring(o),
            )
            for i, o in enumerate((1, -1))
        ]

    for load in slot_loads:
        load.wait()
    r.leaving0[0] = r.cache[a0]
    r.leaving0[1] = r.cache[b0]
    pl.semaphore_wait(barrier, entered)
    tell(here, r.y_in, "y")
    moving0 = [move(r.leaving0, r.arrived0, r.move0_sem, part) for part in range(MOVE_PARTS)]

    loads["lw"].wait()
    r.latents[:, :LAT] = dot_rows(r.tokens[...], r.lw[...])
    copies = [
        send(
            r.latents,
            r.latent_rows.at[o - 1],
            r.latent_sem.at[0, o - 1],
            r.latent_sem.at[1, o - 1],
            here.on_x(lax.rem(here.x + o, N)),
        )
        for o in FAR_FIRST
    ]
    for name in ("queries", "vup", "wo", "wg", "wu", "wd"):
        loads[name].start()
    held = [held_first(r.lengths, moves, me, j) for j in range(ROWS_DEV)]
    held += [held_second(r.lengths, moves, me, j) for j in range(ROWS_DEV)]
    row = lax.broadcasted_iota(jnp.int32, (OWN, 128), 0)
    positions = jnp.zeros((OWN, 128), jnp.int32)
    for i in range(OWN):
        positions = jnp.where(row == i, held[i], positions)

    def held_at(step, place):
        result = held[step * ROWS_DEV]
        for j in range(1, ROWS_DEV):
            result = jnp.where(slots[place] == j, held[step * ROWS_DEV + j], result)
        return result

    held_by_place = [[held_at(step, p) for p in range(ROWS_DEV)] for step in range(STEPS)]
    yield
    hear(here, r.y_in, "y")
    tell(here, r.x_in, "x")
    for copy in copies:
        copy.wait()
    total = r.latents[...]
    for o in range(N - 1):
        total = total + r.latent_rows[o]
    scale = lax.rsqrt(total[:, LAT + 64 :] / D + epsilon)[:, :1]
    content, rotary = fresh_keys(total[:, : LAT + 64] * scale, positions)
    r.fresh[:, :KVR] = content
    r.fresh[:, KVR:] = rotary

    def fresh_row(step, place):
        return r.fresh[pl.ds(step * ROWS_DEV + slots[place], 1), :LAT].astype(jnp.bfloat16)

    loads["queries"].wait()
    r.ordered_copies = []

    def put_out(ref, place):
        copy = pltpu.make_async_copy(ref, r.ordered.at[place], r.out_sem.at[place])
        copy.start()
        r.ordered_copies.append(copy)

    for p in range(EARLY):
        first, second = held_by_place[0][p], held_by_place[1][p]
        block = with_row(r.cache[slots[p]], first, fresh_row(0, p))
        r.early_keys[p] = with_row(block, second, fresh_row(1, p))
        put_out(r.early_keys.at[p], p)
        rows = jnp.concatenate([r.queries[0, slots[p]], r.queries[1, slots[p]]], axis=0)
        step_row = lax.broadcasted_iota(jnp.int32, (2 * HEADS, 1), 0)
        live = jnp.where(step_row < HEADS, first + 1, second + 1)
        result = attend(rows, r.early_keys.at[p], live)
        keep(r, 0, p, result[:HEADS])
        keep(r, 0, EARLY + p, result[HEADS:])

    yield
    hear(here, r.x_in, "x")
    tell(here, r.core_in, "core")
    place_a, place_b = 0, 0
    for p in range(EARLY, ROWS_DEV):
        place_a = jnp.where(slots[p] == a1, p - EARLY, place_a)
        place_b = jnp.where(slots[p] == b1, p - EARLY, place_b)

    def arrive(step, keys, part, arrived, own_a, own_b, kept):
        rows = pl.ds(part * MOVE_ROWS, MOVE_ROWS)
        for p in range(EARLY, ROWS_DEV):
            block = jnp.where(
                slots[p] == own_a,
                arrived[1, rows],
                jnp.where(slots[p] == own_b, arrived[0, rows], kept(p, rows)),
            )
            keys[p - EARLY, rows] = with_row(
                block, held_by_place[step][p] - part * MOVE_ROWS, fresh_row(step, p)
            )

    moving1 = []
    for part in range(MOVE_PARTS):
        rows = pl.ds(part * MOVE_ROWS, MOVE_ROWS)
        for copy in moving0[part]:
            copy.wait()
        arrive(0, r.keys0, part, r.arrived0, a0, b0, lambda p, rows: r.cache[slots[p], rows])
        r.leaving1[0, rows] = r.keys0[place_a, rows]
        r.leaving1[1, rows] = r.keys0[place_b, rows]
        moving1.append(move(r.leaving1, r.arrived1, r.move1_sem, part))
    yield
    loads["vup"].wait()
    hear(here, r.core_in, "core")
    value_up(here, r, 0)
    yield
    for p in range(EARLY, ROWS_DEV):
        keep(
            r, 1, p - EARLY,
            attend(r.queries[0, slots[p]], r.keys0.at[p - EARLY], held_by_place[0][p] + 1),
        )

    yield
    for part in range(MOVE_PARTS):
        for copy in moving1[part]:
            copy.wait()
        arrive(1, r.keys1, part, r.arrived1, a1, b1, lambda p, rows: r.keys0[p - EARLY, rows])
    for p in range(EARLY, ROWS_DEV):
        put_out(r.keys1.at[p - EARLY], p)
        keep(
            r, 1, p,
            attend(r.queries[1, slots[p]], r.keys1.at[p - EARLY], held_by_place[1][p] + 1),
        )
    yield
    value_up(here, r, 1)
    yield


def reduce_over_groups(here, r, step, use):
    own, peer = r.own.at[step], r.peer_rows.at[use, step]
    sem = r.sum_sem.at[use, step]
    sums, rows = r.sums.at[step], r.rows.at[use, step]
    r.core_copy[use, step].wait()
    for o in reversed(CHIPS):
        y, z = here.chip(o)
        k = y * N + z
        sums[k] = (own[k].astype(jnp.float32) + peer[k].astype(jnp.float32)).astype(jnp.bfloat16)
        send(sums.at[k], rows.at[o], sem.at[0, 0], sem.at[1, 0], here.on_chip(y, z))
    k = here.y * N + here.z
    total = own[k].astype(jnp.float32) + peer[k].astype(jnp.float32)
    yield
    arrivals = rows.at[pl.ds(1, BLOCKS - 1)]
    wait_all(arrivals, sem.at[1, 0])
    for o in CHIPS:
        total = total + rows[o].astype(jnp.float32)
    wait_all(arrivals, sem.at[0, 0])
    return total


def project_both(here, r, step, use, lhs, weight):
    project(lhs(1 - here.c), weight, r.to_peer.at[step])
    core_sem = r.core_sem.at[use, step]
    r.core_copy[use, step] = send(
        r.to_peer.at[step], r.peer_rows.at[use, step], core_sem.at[0], core_sem.at[1], here.on_core()
    )
    project(lhs(here.c), weight, r.own.at[step])


def back_line(here, r, step):
    f32, bf16 = jnp.float32, jnp.bfloat16

    pltpu.make_async_copy(r.head_rows.at[step], r.head_rows.at[step], r.head_recv.at[step]).wait()
    rows = r.head_rows[step].astype(f32)
    for h in range(N):
        first = h % 2 * ROWS_DEV
        r.head_block[:, h * HD : (h + 1) * HD] = (
            rows[:, h // 2, first : first + ROWS_DEV].reshape(2 * HALF, HD).astype(bf16)
        )
    if step == 0:
        r.loads["wo"].wait()

    def half(ref, c):
        return ref[pl.ds(pl.multiple_of(c * HALF, HALF), HALF), :]

    project_both(here, r, step, 0, lambda c: half(r.head_block, c), r.wo[...])
    for i in range(ROWS_DEV):
        token = i // EARLY * ROWS_DEV + r.slots[step * EARLY + i % EARLY]
        r.line_tokens[step, i : i + 1, :] = r.tokens_wide[pl.ds(token, 1), :]
    r.mixed[step] = stacked(r.line_tokens[step])[0]
    yield
    attention = yield from reduce_over_groups(here, r, step, 0)
    mixed = (r.mixed[step] + attention).astype(bf16).astype(f32)
    r.mixed[step] = mixed

    mixed_all = r.mixed_all.at[step]
    mine = mixed_all.at[here.c, here.y, here.z]
    mine[...] = mixed.astype(bf16)
    sem, core_sem = r.gather_sem.at[step], r.gather_core.at[step]
    for o in reversed(CHIPS):
        send(mine, mine, sem.at[0, 0], sem.at[1, o // N], here.on_chip(*here.chip(o)))

    @pl.loop(0, GROUPS)
    def _(i):
        kept, copy, _ = head_copy(here, r, step, i)

        @pl.when(jnp.logical_not(kept))
        def _():
            copy().wait_send()

    yield
    handed = []
    for o in (0, *NEAR_FIRST):
        y = lax.rem(here.y + N - o, N)
        block = mixed_all.at[here.c, y]
        wait_all(block if o else mixed_all.at[here.c, y, pl.ds(0, N - 1)], sem.at[1, o])
        handed.append(send(block, block, core_sem.at[0, o], core_sem.at[1, o], here.on_core()))

    wait_all(r.rows.at[0, step, pl.ds(1, BLOCKS - 1)], sem.at[0, 0])

    if step == 0:
        r.loads["wg"].wait()
        r.loads["wu"].wait()
    sums = (
        (r.gate_part.at[step], r.gate_rows.at[step], r.gate_sem.at[step], r.wg),
        (r.up_part.at[step], r.up_rows.at[step], r.up_sem.at[step], r.wu),
    )

    def chunk_copy(part, rows, sem, k):
        slot = lax.rem(k - here.x + N, N) - 1
        return remote(part.at[k], rows.at[slot], sem.at[0, slot], sem.at[1, slot], here.on_x(k))

    for core in (here.c, 1 - here.c):
        if core is not here.c:
            yield
            for copy in handed:
                copy.wait()
        wide = unstacked(mixed_all[core].astype(f32).reshape(BLOCKS, TILE, COLS))
        r.lhs[...] = (wide * r.gain[...].reshape(1, WIDTH)).astype(bf16)
        pieces = in_pieces(jnp.sum(wide * wide, axis=1, keepdims=True))
        for part, rows, sem, weight in sums:
            result = dot_rows(r.lhs[...], weight[...])
            if weight is r.wg:
                lane = lax.broadcasted_iota(jnp.int32, result.shape, 1)
                for i, piece in enumerate(pieces):
                    result = jnp.where(lane == FF_DEV + i, piece, result)
            part[pl.ds(2 * core, 2)] = result.astype(bf16).reshape(2, CHUNK, -1)
            for i in range(2):
                k = 2 * core + lax.rem(here.x + i, 2)

                @pl.when(k != here.x)
                def _():
                    chunk_copy(part, rows, sem, k).start()

    yield
    totals = []
    for part, rows, sem, _ in sums:
        total = part[here.x].astype(f32)
        for o in NEAR_FIRST:
            chunk_copy(part, rows, sem, lax.rem(here.x + o, N)).wait()
        for o in range(N - 1):
            total = total + rows[o].astype(f32)
        totals.append(total)
    gate, up = totals
    lane = lax.broadcasted_iota(jnp.int32, gate.shape, 1)
    squares = jnp.sum(jnp.where(lane >= FF_DEV, gate, 0.0), axis=1, keepdims=True)
    scale = lax.rsqrt(squares / D + epsilon)
    gate, up = gate[:, :FF_DEV] * scale, up * scale
    activation = r.activation.at[step]
    activation[here.x] = (gate / (1.0 + jnp.exp(-gate)) * up).astype(bf16)
    mine = activation.at[here.x]
    sem = r.act_sem.at[step]
    copies = {}
    for o in FAR_FIRST:
        x = lax.rem(here.x + o, N)
        copies[o] = send(mine, mine, sem.at[0, o - 1], sem.at[1, o - 1], here.on_x(x))
    yield
    for o in NEAR_FIRST:
        copies[o].wait()

    if step == 0:
        r.loads["wd"].wait()
    project_both(
        here, r, step, 1, lambda c: activation[pl.ds(2 * c, 2)].reshape(HALF, FF_DEV), r.wd[...]
    )
    yield
    down = yield from reduce_over_groups(here, r, step, 1)
    r.results[step * ROWS_DEV : (step + 1) * ROWS_DEV, :] = unstacked((r.mixed[step] + down)[None])
    yield


ORDER = "FFFFF00FF0110010110010111"

INPUTS = (
    "lengths", "moves", "tokens", "gain", "lw_hbm", "queries_hbm", "cache_hbm", "vup_hbm",
    "wo_hbm", "wg_hbm", "wu_hbm", "wd_hbm",
)


def layer_kernel(names, *refs):
    r = types.SimpleNamespace(**dict(zip(names, refs)))
    r.core_copy = {}
    here = Place()
    lines = {"F": front_line(here, r), "0": back_line(here, r, 0), "1": back_line(here, r, 1)}
    for name in ORDER:
        next(lines[name], None)
    for i in range(OWN):
        place = r.places[i % ROWS_DEV]
        row = place // EARLY * ROWS_DEV + i // ROWS_DEV * EARLY + lax.rem(place, EARLY)
        r.sorted_results[i : i + 1, :] = r.results[pl.ds(row, 1), :]
    r.out[...] = r.sorted_results[...].astype(jnp.bfloat16)
    for copy in r.ordered_copies:
        copy.wait()


def layer(lengths, moves, tokens, gain, lw, queries, cache, vup, wo, wg, wu, wd):
    bf16, f32 = jnp.bfloat16, jnp.float32
    vmem = pl.BlockSpec(memory_space=pltpu.VMEM)
    smem = pl.BlockSpec(memory_space=pltpu.SMEM)
    hbm = pl.BlockSpec(memory_space=pl.ANY)
    slot = cache.shape[1:]

    def dma(*shape):
        return pltpu.SemaphoreType.DMA(shape)

    def held(*shape, dtype=bf16):
        return pltpu.VMEM(shape, dtype)

    scratch = dict(
        cache=held(*cache.shape),
        lw=held(*lw.shape),
        queries=held(*queries.shape),
        vup=held(*vup.shape),
        wo=held(*wo.shape),
        wg=held(FF_DEV + SPARE, WIDTH),
        wu=held(*wu.shape),
        wd=held(*wd.shape),
        latents=held(OWN, LAT + 64 + 128, dtype=f32),
        latent_rows=held(N - 1, OWN, LAT + 64 + 128, dtype=f32),
        fresh=held(OWN, LAT + 64, dtype=f32),
        leaving0=held(2, *slot),
        leaving1=held(2, *slot),
        arrived0=held(2, *slot),
        arrived1=held(2, *slot),
        early_keys=held(EARLY, *slot),
        keys0=held(ROWS_DEV - EARLY, *slot),
        keys1=held(ROWS_DEV - EARLY, *slot),
        head_latent=held(2, KVR // 128, ROWS_DEV * HEADS, 128, dtype=f32),
        heads=held(STEPS, 2 * N, N // 2, TILE, HD),
        head_rows=held(STEPS, GROUPS, N // 2, TILE, HD),
        head_block=held(2 * HALF, N * HD),
        to_peer=held(STEPS, BLOCKS, TILE, COLS),
        own=held(STEPS, BLOCKS, TILE, COLS),
        peer_rows=held(2, STEPS, BLOCKS, TILE, COLS),
        sums=held(STEPS, BLOCKS, TILE, COLS),
        rows=held(2, STEPS, BLOCKS, TILE, COLS),
        mixed=held(STEPS, TILE, COLS, dtype=f32),
        mixed_all=held(STEPS, 2, N, N, TILE, COLS),
        lhs=held(HALF, WIDTH),
        gate_part=held(STEPS, N, CHUNK, FF_DEV + SPARE),
        up_part=held(STEPS, N, CHUNK, FF_DEV),
        gate_rows=held(STEPS, N - 1, CHUNK, FF_DEV + SPARE),
        up_rows=held(STEPS, N - 1, CHUNK, FF_DEV),
        activation=held(STEPS, N, CHUNK, FF_DEV),
        results=held(OWN, WIDTH, dtype=f32),
        sorted_results=held(OWN, WIDTH, dtype=f32),
        tokens_wide=held(OWN, WIDTH, dtype=f32),
        line_tokens=held(2, ROWS_DEV, WIDTH, dtype=f32),
        y_in=pltpu.SemaphoreType.REGULAR,
        x_in=pltpu.SemaphoreType.REGULAR,
        core_in=pltpu.SemaphoreType.REGULAR,
        load_sem=dma(7),
        cache_sem=dma(ROWS_DEV),
        latent_sem=dma(2, N - 1),
        move0_sem=dma(2, 2, MOVE_PARTS),
        move1_sem=dma(2, 2, MOVE_PARTS),
        out_sem=dma(ROWS_DEV),
        head_send=dma(STEPS, GROUPS),
        head_recv=dma(STEPS),
        core_sem=dma(2, STEPS, 2),
        sum_sem=dma(2, STEPS, 2, BLOCKS),
        gather_sem=dma(STEPS, 2, BLOCKS),
        gather_core=dma(STEPS, 2, N),
        gate_sem=dma(STEPS, 2, N - 1),
        up_sem=dma(STEPS, 2, N - 1),
        act_sem=dma(STEPS, 2, N - 1),
    )
    names = (*INPUTS, "out", "ordered", *scratch)

    def kernel(*refs):
        layer_kernel(names, *refs)

    return pl.pallas_call(
        kernel,
        out_shape=(
            jax.ShapeDtypeStruct((OWN, WIDTH), bf16),
            jax.ShapeDtypeStruct(cache.shape, bf16),
        ),
        in_specs=[smem, smem, vmem, vmem] + [hbm] * 8,
        out_specs=(vmem, hbm),
        scratch_shapes=list(scratch.values()),
        compiler_params=pltpu.CompilerParams(
            collective_id=0, has_side_effects=True, vmem_limit_bytes=58 * 1024 * 1024
        ),
        name="layer",
    )(lengths, moves, tokens, gain, lw, queries, cache, vup, wo, wg, wu, wd)


def finish_kernel(
    lengths, moves, group, ordered, rows, final_cache, final_rows, final_lengths, moved, slots, row_block, sems, row_sem
):
    _, places = slot_order(moves, group[0])
    loads = [pltpu.make_async_copy(ordered.at[places[j]], slots.at[j], sems.at[0, j]) for j in range(ROWS_DEV)]
    stores = [pltpu.make_async_copy(slots.at[j], final_cache.at[j], sems.at[1, j]) for j in range(ROWS_DEV)]
    loads.append(pltpu.make_async_copy(rows, row_block, row_sem.at[0]))
    stores.append(pltpu.make_async_copy(row_block, final_rows, row_sem.at[1]))
    for load in loads:
        load.start()

    def pass_on(first, last):
        for load, store in zip(loads[first:last], stores[first:last]):
            load.wait()
            store.start()

    @pl.loop(0, GROUPS)
    def _(g):
        for j in range(ROWS_DEV):
            moved[g * ROWS_DEV + j] = lengths[g * ROWS_DEV + j] + 1

    pass_on(0, 3)

    @pl.loop(0, GROUPS)
    def _(g):
        right = lax.rem(g + 1, GROUPS)
        left = lax.rem(g + GROUPS - 1, GROUPS)
        moved[g * ROWS_DEV + moves[0, 0, g]] = lengths[right * ROWS_DEV + moves[0, 1, right]] + 1
        moved[g * ROWS_DEV + moves[0, 1, g]] = lengths[left * ROWS_DEV + moves[0, 0, left]] + 1

    pass_on(3, ROWS_DEV + 1)

    @pl.loop(0, GROUPS)
    def _(g):
        for j in range(ROWS_DEV):
            final_lengths[g * ROWS_DEV + j] = moved[g * ROWS_DEV + j] + 1

    @pl.loop(0, GROUPS)
    def _(g):
        right = lax.rem(g + 1, GROUPS)
        left = lax.rem(g + GROUPS - 1, GROUPS)
        final_lengths[g * ROWS_DEV + moves[1, 0, g]] = moved[right * ROWS_DEV + moves[1, 1, right]] + 1
        final_lengths[g * ROWS_DEV + moves[1, 1, g]] = moved[left * ROWS_DEV + moves[1, 0, left]] + 1

    for store in stores:
        store.wait()


def finish(lengths, moves, group, ordered, rows):
    smem = pl.BlockSpec(memory_space=pltpu.SMEM)
    hbm = pl.BlockSpec(memory_space=pltpu.HBM)
    return pl.pallas_call(
        finish_kernel,
        out_shape=(
            jax.ShapeDtypeStruct(ordered.shape, ordered.dtype),
            jax.ShapeDtypeStruct(rows.shape, rows.dtype),
            jax.ShapeDtypeStruct(lengths.shape, jnp.int32),
        ),
        in_specs=[smem, smem, smem, hbm, hbm],
        out_specs=(hbm, hbm, smem),
        scratch_shapes=[
            pltpu.SMEM(lengths.shape, jnp.int32),
            pltpu.VMEM(ordered.shape, ordered.dtype),
            pltpu.VMEM(rows.shape, rows.dtype),
            pltpu.SemaphoreType.DMA((2, ROWS_DEV)),
            pltpu.SemaphoreType.DMA((2,)),
        ],
        compiler_params=pltpu.CompilerParams(vmem_limit_bytes=60 * 1024 * 1024),
        name="finish",
    )(lengths, moves, group, ordered, rows)


def on_device(
    latent_cache,
    lengths,
    slot_moves,
    hidden_in,
    queries,
    latent_weight,
    value_up_projection,
    out_weight,
    post_gain,
    gate_projection_matrix,
    up_weight,
    down_weight,
):
    moves = jnp.swapaxes(slot_moves, 1, 2)
    rows, ordered = layer(
        lengths,
        moves,
        hidden_in.reshape(OWN, WIDTH),
        post_gain,
        latent_weight.T,
        queries,
        latent_cache,
        value_up_projection,
        out_weight,
        gate_projection_matrix.T,
        up_weight.T,
        down_weight,
    )
    group = lax.axis_index("dp").reshape(1)
    final_cache, final_rows, final_lengths = finish(lengths, moves, group, ordered, rows)
    return (final_rows.reshape(STEPS, ROWS_DEV, WIDTH), final_cache, final_lengths)


def solution(mesh):
    return jax.shard_map(
        on_device,
        mesh=mesh,
        in_specs=(
            P("dp", None, None),
            P(),
            P(),
            P(None, "dp", "tp"),
            P(None, "dp", "tp", None),
            P("tp", None),
            P("tp", None, None),
            P("dp", "tp"),
            P("tp"),
            P("tp", "dp"),
            P("tp", "dp"),
            P("dp", "tp"),
        ),
        out_specs=(P(None, "dp", "tp"), P("dp", None, None), P()),
        check_vma=False,
    )
```
